256 devices in a mesh: space: 32 (over z, y), snap: 8 (over x, core).
Axes of the slice: x: 4, y: 4, z: 8, core: 2. Of those that a mesh axis runs over, the one named last changes fastest.
Arguments:
- snaps: bfloat16 [512, 1048576], P('snap', 'space'), may hold values from -50 to 50
- sketch: bfloat16 [32, 512], P(None, 'snap'), may hold values from -0.75 to 0.75
- merge_mix: float32 [64, 32], replicated, may hold values from -0.75 to 0.75
Outputs:
- basis: float32 [32, 1048576], P('snap', 'space')
The draws below stay inside these ranges and needn't reach their ends.
All inputs are finite; a program needn't handle non-finite values.
Results may differ from the reference program's by a relative error of at most 0.0075.
Values may be sent and summed in bfloat16 or wider, within the bound.
No kernel may reach another device: no remote copies, remote signals or barrier semaphores. Data moves between devices by JAX's collectives and lax.ppermute only.
A program may use at most 64 MiB of HBM per device.

```python
import math
import jax
import jax.numpy as jnp
from jax import lax

SNAP_DEV = 64
K = 32
ITERS = 4
NPTS = 1048576
NSNAP = 512
N_SNAP = 8


def draw_snaps(key, part):
    key = jax.random.fold_in(key, 11)
    keys = jax.random.split(key, 7)
    shared_count = K // 2
    coeff_scale = math.sqrt(5.0 / K)
    snap_scale = jnp.exp(jax.random.uniform(keys[2], (NSNAP, 1), jnp.float32) * math.log(3.0))
    base = jax.random.truncated_normal(keys[0], -5.0, 5.0, (NSNAP, NPTS), jnp.float32)
    fields = jax.random.truncated_normal(keys[5], -4.0, 4.0, (shared_count, NPTS), jnp.float32)
    weights = coeff_scale * jax.random.truncated_normal(keys[6], -3.0, 3.0, (NSNAP, shared_count), jnp.float32)
    point_scale = jnp.exp(jax.random.uniform(keys[1], (1, NPTS), jnp.float32) * math.log(10.0))
    divisor = 5.0
    shared = jnp.zeros((NSNAP, NPTS), jnp.float32)
    for mode_index in range(shared_count):
        shared = shared + weights[:, mode_index:mode_index + 1] * fields[mode_index:mode_index + 1, :]
    values = (base + shared) * point_scale * snap_scale / divisor
    return jnp.clip(values, -50.0, 50.0).astype(jnp.bfloat16)


def shard_levels(key, shape, cuts, least, high):
    level = 1.0
    for position, shards_of in cuts:
        draws = jax.random.uniform(jax.random.fold_in(jax.random.fold_in(key, 6), position), (shards_of,), jnp.float32, least / len(cuts), high / len(cuts))
        level = level * jnp.repeat(jnp.exp(draws), shape[position] // shards_of).reshape((-1,) + (1,) * (len(shape) - 1 - position))
    return level


def gaussian(key, shape, scale, limit, shards=(), kind=jnp.bfloat16):
    values = scale * jax.random.normal(key, shape, jnp.float32)
    if shards:
        values = values * shard_levels(key, shape, shards, -0.22, 0.18)
    return jnp.clip(values, -limit, limit).astype(kind)


def setup_inputs(seed: int = 0) -> dict:
    streams_of = jax.random.split(jax.random.key(seed), 4)
    snaps = draw_snaps(jax.random.fold_in(streams_of[3], 71), 0)
    sketch = gaussian(streams_of[1], (K, NSNAP), SNAP_DEV ** -0.5, 0.75, ((1, 8),))
    merge_mix = gaussian(streams_of[2], (2 * K, K), (2 * K) ** -0.5, 0.75, (), jnp.float32)
    return dict(snaps=snaps, sketch=sketch, merge_mix=merge_mix)


def make_mixing(gram_matrix, merge_mix):
    curved = jnp.dot(gram_matrix, merge_mix, precision=lax.Precision.HIGHEST)
    small_matrix = jnp.dot(merge_mix.T, curved, precision=lax.Precision.HIGHEST)
    factor = jnp.linalg.cholesky(small_matrix)
    scale = 1.0 / jnp.sqrt(jnp.trace(gram_matrix))
    return jax.scipy.linalg.solve_triangular(factor, curved.T, lower=True) * scale

def power_block(block, test_block):
    current = jnp.dot(test_block.astype(jnp.float32), block.astype(jnp.float32), preferred_element_type=jnp.float32).astype(jnp.bfloat16)
    scale = 1.0 / math.sqrt(SNAP_DEV)
    for sweep_index in range(ITERS):
        weighted = lax.dot_general(block.astype(jnp.float32), current.astype(jnp.float32), (((1,), (1,)), ((), ())), preferred_element_type=jnp.float32)
        inner = lax.dot_general(current.astype(jnp.float32), current.astype(jnp.float32), (((1,), (1,)), ((), ())), preferred_element_type=jnp.float32)
        factor = jnp.linalg.cholesky(inner)
        coeffs = jax.scipy.linalg.solve_triangular(factor, weighted.T, lower=True).astype(jnp.bfloat16)
        current = (jnp.dot(coeffs.astype(jnp.float32), block.astype(jnp.float32), preferred_element_type=jnp.float32) * scale).astype(jnp.bfloat16)
    return current

def reference(snaps, sketch, merge_mix):
    pieces = []
    for block_index in range(N_SNAP):
        lower_row = block_index * SNAP_DEV
        block = snaps[lower_row:lower_row + SNAP_DEV]
        test_block = sketch[:, lower_row:lower_row + SNAP_DEV]
        pieces.append(power_block(block, test_block))
    while len(pieces) > 1:
        merged = []
        for pair_index in range(len(pieces) // 2):
            stacked = jnp.concatenate([pieces[2 * pair_index].astype(jnp.float32), pieces[2 * pair_index + 1].astype(jnp.float32)], axis=0)
            gram_matrix = jnp.dot(stacked, stacked.T, precision=lax.Precision.HIGHEST)
            mixing = make_mixing(gram_matrix, merge_mix)
            merged.append(jnp.dot(mixing, stacked, precision=lax.Precision.HIGHEST))
        pieces = merged
    return pieces[0]
```

```python
import functools
import math

import jax
import jax.numpy as jnp
from jax import lax
from jax.experimental import pallas as pl
from jax.experimental.pallas import tpu as pltpu
from jax.sharding import PartitionSpec as P

ITERS = 4
F32 = jnp.float32
BF16 = jnp.bfloat16
VMEM_LIMIT = 48 * 1024 * 1024


def dot_nn(a, b):
    return jnp.dot(a, b, precision=lax.Precision.HIGHEST, preferred_element_type=F32)


def dot_nt(a, b):
    return lax.dot_general(
        a, b, (((1,), (1,)), ((), ())), precision=lax.Precision.HIGHEST, preferred_element_type=F32
    )


def dot_tn(a, b):
    return lax.dot_general(
        a, b, (((0,), (0,)), ((), ())), precision=lax.Precision.HIGHEST, preferred_element_type=F32
    )


def cholesky_solves(pairs):
    modes = pairs[0][0].shape[0]
    tables = []
    for h, b in pairs:
        table = jnp.concatenate([b, h], axis=1)
        tables.append([table[r : r + 8] for r in range(0, modes, 8)])
    wide = pairs[0][1].shape[1]
    row_ids = lax.broadcasted_iota(jnp.int32, (8, 1), 0)
    for j in range(modes):
        group, inner = divmod(j, 8)
        for table in tables:
            row = table[group][inner : inner + 1]
            pivot_row = row * (1.0 / row[:, wide + j : wide + j + 1])
            for g in range(group, modes // 8):
                column = table[g][:, wide + j : wide + j + 1]
                if g == group:
                    column = jnp.where(row_ids > inner, column, 0.0)
                table[g] = table[g] - column * pivot_row
    solved = []
    for table in tables:
        whole = jnp.concatenate(table, axis=0)
        below = whole[:, wide:]
        same = lax.broadcasted_iota(jnp.int32, below.shape, 0) == lax.broadcasted_iota(
            jnp.int32, below.shape, 1
        )
        diagonal = jnp.sum(jnp.where(same, below, 0.0), axis=1, keepdims=True)
        solved.append(whole[:, :wide] * lax.rsqrt(diagonal))
    return solved


def trace_scale(gram):
    same = lax.broadcasted_iota(jnp.int32, gram.shape, 0) == lax.broadcasted_iota(
        jnp.int32, gram.shape, 1
    )
    diagonal = jnp.where(same, gram, 0.0)
    return lax.rsqrt(jnp.sum(jnp.sum(diagonal, axis=1, keepdims=True), axis=0, keepdims=True))


def mixings(grams, mix):
    pairs = []
    for gram in grams:
        curved_t = dot_tn(mix, gram)
        pairs.append((dot_nn(curved_t, mix), curved_t))
    return [s * trace_scale(g) for s, g in zip(cholesky_solves(pairs), grams)]


def split_two(x):
    high = x.astype(BF16)
    return jnp.concatenate([high, (x - high.astype(F32)).astype(BF16)], axis=0)


def apply_mixing(split, rows):
    both = jnp.dot(split, rows, preferred_element_type=F32)
    modes = split.shape[0] // 2
    return both[:modes] + both[modes:]


def pack_kernel(core_ref, rows_ref, out_ref):
    out_ref[...] = rows_ref[...]


def gram_pair_kernel(core_ref, mine_ref, other_ref, gram_ref, total_ref):
    step = pl.program_id(0)
    rows = jnp.concatenate([mine_ref[...], other_ref[...]], axis=0)
    part = lax.dot_general(
        rows, rows, (((1,), (1,)), ((), ())), preferred_element_type=F32
    )

    @pl.when(step == 0)
    def _():
        total_ref[...] = part

    @pl.when(step > 0)
    def _():
        total_ref[...] += part

    @pl.when(step == pl.num_programs(0) - 1)
    def _():
        total = total_ref[...]
        half = total.shape[0] // 2
        swapped = pltpu.roll(pltpu.roll(total, half, 0), half, 1)
        gram_ref[...] = jnp.where(core_ref[0] == 0, total, swapped)


def power_merge_kernel(core_ref, gram_ref, sk_mine_ref, sk_other_ref, mix_ref, mine_ref, other_ref, piece_ref, split_ref):
    step = pl.program_id(0)

    @pl.when(step == 0)
    def _():
        first = core_ref[0] == 0
        gram = gram_ref[...]
        width = gram.shape[0] // 2
        scale = 1.0 / math.sqrt(width)
        sk_mine = sk_mine_ref[...].astype(F32)
        sk_other = sk_other_ref[...].astype(F32)
        coeffs = [jnp.where(first, sk_mine, sk_other), jnp.where(first, sk_other, sk_mine)]
        grams = [gram[:width, :width], gram[width:, width:]]
        for _ in range(ITERS):
            pairs = []
            for a, g in zip(coeffs, grams):
                weighted = dot_nn(a, g)
                pairs.append((dot_nt(weighted, a), weighted))
            coeffs = [c.astype(BF16).astype(F32) * scale for c in cholesky_solves(pairs)]
        modes = coeffs[0].shape[0]
        zero = jnp.zeros((modes, width), F32)
        both = jnp.concatenate(
            [jnp.concatenate([coeffs[0], zero], axis=1), jnp.concatenate([zero, coeffs[1]], axis=1)],
            axis=0,
        )
        stacked_gram = dot_nt(dot_nn(both, gram), both)
        mixing = dot_nn(mixings([stacked_gram], mix_ref[...])[0], both)
        mixing = jnp.where(first, mixing, pltpu.roll(mixing, width, 1))
        split_ref[...] = split_two(mixing)

    rows = jnp.concatenate([mine_ref[...], other_ref[...]], axis=0)
    piece_ref[0] = apply_mixing(split_ref[...], rows).astype(BF16)


def gram_kernel(rows_ref, gram_ref):
    rows = rows_ref[...]
    gram_ref[...] = lax.dot_general(
        rows, rows, (((1,), (1,)), ((), ())), preferred_element_type=F32
    )


def tree_kernel(gram_ref, mix_ref, rows_ref, out_ref):
    gram = gram_ref[...]
    mix = mix_ref[...]
    pair = mix.shape[0]
    modes = mix.shape[1]
    count = gram.shape[0] // modes
    whole = None
    while count > 1:
        blocks = [gram[i * pair : (i + 1) * pair, i * pair : (i + 1) * pair] for i in range(count // 2)]
        made = mixings(blocks, mix)
        count //= 2
        if count == 1:
            step = made[0]
        else:
            step = jnp.concatenate(
                [
                    jnp.concatenate(
                        [m if i == k else jnp.zeros_like(m) for k in range(count)], axis=1
                    )
                    for i, m in enumerate(made)
                ],
                axis=0,
            )
        whole = step if whole is None else dot_nn(step, whole)
        if count > 1:
            gram = dot_nt(dot_nn(step, gram), step)
    result = apply_mixing(split_two(whole), rows_ref[...])
    own = modes // out_ref.shape[0]
    for i in range(out_ref.shape[0]):
        out_ref[i] = result[i * own : (i + 1) * own].astype(BF16)


def params():
    return pltpu.CompilerParams(vmem_limit_bytes=VMEM_LIMIT)


def swap(block, axis, mask):
    count = lax.axis_size(axis)
    return lax.ppermute(block, axis, [(i, i ^ mask) for i in range(count)])


def butterfly(block, steps):
    for axis, mask in steps:
        block = block + swap(block, axis, mask)
    return block


SPACE_STEPS = [("space", 1), ("space", 3), ("space", 4), ("space", 8), ("space", 24)]
CORE_STEPS = [("snap", 1)]
X_STEPS = [("snap", 2), ("snap", 6)]


def shards(snaps, sketch, merge_mix):
    width, points = snaps.shape
    modes = sketch.shape[0]
    snap_count = lax.axis_size("snap")
    chunk = points // snap_count
    chips = snap_count // 2
    own_modes = modes // snap_count
    core = lax.axis_index("snap") % 2
    core_ref = core.reshape(1).astype(jnp.int32)

    away = pl.pallas_call(
        pack_kernel,
        out_shape=jax.ShapeDtypeStruct((width, chips * chunk), snaps.dtype),
        grid_spec=pltpu.PrefetchScalarGridSpec(
            num_scalar_prefetch=1,
            grid=(chips,),
            in_specs=[pl.BlockSpec((width, chunk), lambda i, c: (0, 2 * i + 1 - c[0]))],
            out_specs=pl.BlockSpec((width, chunk), lambda i, c: (0, i)),
        ),
        compiler_params=params(),
        name="pack",
    )(core_ref, snaps)
    other = swap(away, "snap", 1)
    sk_other = swap(sketch, "snap", 1)

    mine_spec = pl.BlockSpec((width, chunk), lambda i, c: (0, 2 * i + c[0]))
    other_spec = pl.BlockSpec((width, chunk), lambda i, c: (0, i))
    full = lambda shape: pl.BlockSpec(shape, lambda i, c: (0,) * len(shape))

    gram = pl.pallas_call(
        gram_pair_kernel,
        out_shape=jax.ShapeDtypeStruct((2 * width, 2 * width), F32),
        grid_spec=pltpu.PrefetchScalarGridSpec(
            num_scalar_prefetch=1,
            grid=(chips,),
            in_specs=[mine_spec, other_spec],
            out_specs=full((2 * width, 2 * width)),
            scratch_shapes=[pltpu.VMEM((2 * width, 2 * width), F32)],
        ),
        compiler_params=params(),
        name="gram_pair",
    )(core_ref, snaps, other)
    gram = butterfly(gram, CORE_STEPS + SPACE_STEPS)

    piece = pl.pallas_call(
        power_merge_kernel,
        out_shape=jax.ShapeDtypeStruct((chips, modes, chunk), BF16),
        grid_spec=pltpu.PrefetchScalarGridSpec(
            num_scalar_prefetch=1,
            grid=(chips,),
            in_specs=[
                full((2 * width, 2 * width)),
                full(sketch.shape),
                full(sketch.shape),
                full(merge_mix.shape),
                mine_spec,
                other_spec,
            ],
            out_specs=pl.BlockSpec((1, modes, chunk), lambda i, c: (i, 0, 0)),
            scratch_shapes=[pltpu.VMEM((2 * modes, 2 * width), BF16)],
        ),
        compiler_params=params(),
        name="power_merge",
    )(core_ref, gram, sketch, sk_other, merge_mix, snaps, other)

    groups = [[2 * x + c for x in range(chips)] for c in range(2)]
    rows = lax.all_to_all(piece, "snap", 0, 0, tiled=True, axis_index_groups=groups)
    rows = rows.reshape(chips * modes, chunk)

    vmem = pl.BlockSpec(memory_space=pltpu.VMEM)
    gram = pl.pallas_call(
        gram_kernel,
        out_shape=jax.ShapeDtypeStruct((chips * modes, chips * modes), F32),
        in_specs=[vmem],
        out_specs=vmem,
        compiler_params=params(),
        name="gram_rows",
    )(rows)
    gram = butterfly(gram, CORE_STEPS + X_STEPS + SPACE_STEPS)

    merged = pl.pallas_call(
        tree_kernel,
        out_shape=jax.ShapeDtypeStruct((snap_count, own_modes, chunk), BF16),
        in_specs=[vmem] * 3,
        out_specs=vmem,
        compiler_params=params(),
        name="tree",
    )(gram, merge_mix, rows)

    basis = lax.all_to_all(merged, "snap", 0, 0, tiled=True)
    return basis.transpose(1, 0, 2).reshape(own_modes, points).astype(F32)


def solution(mesh):
    in_specs = (P("snap", "space"), P(None, "snap"), P())
    out_specs = P("snap", "space")
    return jax.shard_map(shards, mesh=mesh, in_specs=in_specs, out_specs=out_specs, check_vma=False)
```

```python
import functools
import math

import jax
import jax.numpy as jnp
from jax import lax
from jax.experimental import pallas as pl
from jax.experimental.pallas import tpu as pltpu
from jax.sharding import PartitionSpec as P

ITERS = 4
PANEL = 8
F32 = jnp.float32
BF16 = jnp.bfloat16
VMEM_LIMIT = 48 * 1024 * 1024


def dot_nn(a, b):
    return jnp.dot(a, b, precision=lax.Precision.HIGHEST, preferred_element_type=F32)


def dot_nt(a, b):
    return lax.dot_general(
        a, b, (((1,), (1,)), ((), ())), precision=lax.Precision.HIGHEST, preferred_element_type=F32
    )


def dot_tn(a, b):
    return lax.dot_general(
        a, b, (((0,), (0,)), ((), ())), precision=lax.Precision.HIGHEST, preferred_element_type=F32
    )


def eliminate_panel(table, wide, first):
    group, inner = divmod(first, 8)
    shape = table[0].shape
    row_ids = lax.broadcasted_iota(jnp.int32, shape, 0)
    columns = [
        [jnp.broadcast_to(t[:, wide + first + k : wide + first + k + 1], shape) for t in table[group:]]
        for k in range(PANEL)
    ]
    rows = [jnp.broadcast_to(table[group][inner + k : inner + k + 1], shape) for k in range(PANEL)]
    corner = {
        (k, l): jnp.broadcast_to(columns[k][0][inner + l : inner + l + 1], shape)
        for k in range(PANEL)
        for l in range(k, PANEL)
    }
    for k in range(PANEL):
        inverse = 1.0 / corner[k, k]
        factors = [c * inverse for c in columns[k]]
        steps = {l: corner[k, l] * inverse for l in range(k + 1, PANEL)}
        for l in range(k + 1, PANEL):
            for m in range(l, PANEL):
                corner[l, m] = corner[l, m] - steps[l] * corner[k, m]
            columns[l] = [c - f * corner[k, l] for c, f in zip(columns[l], factors)]
            rows[l] = rows[l] - steps[l] * rows[k]
        factors[0] = jnp.where(row_ids > inner + k, factors[0], 0.0)
        for g, f in enumerate(factors):
            table[group + g] = table[group + g] - f * rows[k]


def cholesky_solves(pairs):
    modes = pairs[0][0].shape[0]
    wide = pairs[0][1].shape[1]
    tables = []
    for h, b in pairs:
        table = jnp.concatenate([b, h], axis=1)
        tables.append([table[r : r + 8] for r in range(0, modes, 8)])
    for first in range(0, modes, PANEL):
        for table in tables:
            eliminate_panel(table, wide, first)
    solved = []
    for table in tables:
        whole = jnp.concatenate(table, axis=0)
        below = whole[:, wide:]
        same = lax.broadcasted_iota(jnp.int32, below.shape, 0) == lax.broadcasted_iota(
            jnp.int32, below.shape, 1
        )
        diagonal = jnp.sum(jnp.where(same, below, 0.0), axis=1, keepdims=True)
        solved.append(whole[:, :wide] * lax.rsqrt(diagonal))
    return solved


def trace_scale(gram):
    same = lax.broadcasted_iota(jnp.int32, gram.shape, 0) == lax.broadcasted_iota(
        jnp.int32, gram.shape, 1
    )
    diagonal = jnp.where(same, gram, 0.0)
    return lax.rsqrt(jnp.sum(jnp.sum(diagonal, axis=1, keepdims=True), axis=0, keepdims=True))


def mixings(grams, mix):
    pairs = []
    for gram in grams:
        curved_t = dot_tn(mix, gram)
        pairs.append((dot_nn(curved_t, mix), curved_t))
    return [s * trace_scale(g) for s, g in zip(cholesky_solves(pairs), grams)]


def split_two(x):
    high = x.astype(BF16)
    return jnp.concatenate([high, (x - high.astype(F32)).astype(BF16)], axis=0)


def bf16_dot(a, b):
    return jnp.dot(a, b, preferred_element_type=F32)


def bf16_dot_nt(a, b):
    return lax.dot_general(a, b, (((1,), (1,)), ((), ())), preferred_element_type=F32)


def joined(both):
    modes = both.shape[0] // 2
    return both[:modes] + both[modes:]


def own_gram_kernel(place_ref, snaps_ref, gram_ref, mine_ref, away_ref, sems):
    core = place_ref[0]
    width, points = mine_ref.shape
    chips = sems.shape[0] // 2
    chunk = points // chips
    copies = []
    for i in range(chips):
        here = pl.ds(i * chunk, chunk)
        for packed_ref, parity in ((mine_ref, core), (away_ref, 1 - core)):
            there = pl.ds(pl.multiple_of((2 * i + parity) * chunk, chunk), chunk)
            copies.append(
                pltpu.make_async_copy(snaps_ref.at[:, there], packed_ref.at[:, here], sems.at[len(copies)])
            )
    for copy in copies:
        copy.start()
    total = jnp.zeros((width, width), F32)
    for k, copy in enumerate(copies):
        copy.wait()
        i, packed_ref = k // 2, (mine_ref, away_ref)[k % 2]
        rows = packed_ref[:, i * chunk : (i + 1) * chunk]
        total += bf16_dot_nt(rows, rows)
    gram_ref[...] = jnp.zeros_like(gram_ref)
    gram_ref[:, :width] = total


def cross_gram_kernel(place_ref, mine_ref, other_ref, gram_ref):
    width = mine_ref.shape[0]
    gram_ref[...] = jnp.zeros_like(gram_ref)

    @pl.when(place_ref[0] == 0)
    def _():
        gram_ref[:, width:] = bf16_dot_nt(mine_ref[...], other_ref[...])

    @pl.when(place_ref[0] != 0)
    def _():
        gram_ref[:, width:] = bf16_dot_nt(other_ref[...], mine_ref[...])


def power_kernel(iters, last, gram_ref, coeffs_ref, out_ref):
    coeffs = coeffs_ref[...].astype(F32)
    width = coeffs.shape[1]
    modes = coeffs.shape[0]
    gram = gram_ref[:, :width]
    scale = 1.0 / math.sqrt(width)
    for _ in range(iters):
        weighted = dot_nn(coeffs, gram)
        solved = cholesky_solves([(dot_nt(weighted, coeffs), weighted)])[0]
        coeffs = solved.astype(BF16).astype(F32) * scale
    if last:
        out_ref[...] = jnp.zeros_like(out_ref)
        out_ref[:, :width] = coeffs
        out_ref[:, width : width + modes] = dot_nt(dot_nn(coeffs, gram), coeffs)
    else:
        out_ref[...] = coeffs


def stack_gram(low, cross, cross_t, high):
    return jnp.concatenate(
        [jnp.concatenate([low, cross], axis=1), jnp.concatenate([cross_t, high], axis=1)], axis=0
    )


def merge_kernel(place_ref, cross_ref, mine_co_ref, other_co_ref, mix_ref, mine_ref, other_ref, *piece_refs):
    first = place_ref[0] == 0
    width = mine_ref.shape[0]
    modes = mine_co_ref.shape[0]
    mine_co, other_co = mine_co_ref[...], other_co_ref[...]
    low = jnp.where(first, mine_co, other_co)
    high = jnp.where(first, other_co, mine_co)
    low_co, high_co = low[:, :width], high[:, :width]
    cross = cross_ref[:, width:]
    gram = stack_gram(
        low[:, width : width + modes],
        dot_nt(dot_nn(low_co, cross), high_co),
        dot_nt(dot_nt(high_co, cross), low_co),
        high[:, width : width + modes],
    )
    mixing = mixings([gram], mix_ref[...])[0]
    low_mix = dot_nn(mixing[:, :modes], low_co)
    high_mix = dot_nn(mixing[:, modes:], high_co)
    mine_split = split_two(jnp.where(first, low_mix, high_mix))
    other_split = split_two(jnp.where(first, high_mix, low_mix))
    chunk = piece_refs[0].shape[1]
    for i, piece_ref in enumerate(piece_refs):
        here = pl.ds(pl.multiple_of((place_ref[1] ^ i) * chunk, chunk), chunk)
        both = bf16_dot(mine_split, mine_ref[:, here]) + bf16_dot(other_split, other_ref[:, here])
        piece_ref[...] = joined(both).astype(BF16)


def rows_gram_kernel(place_ref, *refs):
    piece_refs, (rows_ref, gram_ref) = refs[:-2], refs[-2:]
    modes = piece_refs[0].shape[0]
    for i, piece_ref in enumerate(piece_refs):
        start = pl.multiple_of((place_ref[1] ^ i) * modes, modes)
        rows_ref[pl.ds(start, modes), :] = piece_ref[...]
    rows = rows_ref[...]
    gram = bf16_dot_nt(rows, rows)
    m, h = modes, modes // 2
    gram_ref[:m] = gram[:m]
    gram_ref[m : 2 * m] = gram[m : 2 * m]
    gram_ref[m : 2 * m, :m] = gram[3 * m :, 3 * m :]
    gram_ref[2 * m :, : 2 * m] = gram[2 * m : 2 * m + h, 2 * m :]
    gram_ref[2 * m :, 2 * m :] = gram[2 * m + h : 3 * m, 2 * m :]


def tree_kernel(gram_ref, mix_ref, rows_ref, out_ref):
    mix = mix_ref[...]
    m = mix.shape[1]
    h = m // 2
    top = gram_ref[:m]
    second = gram_ref[m : 2 * m]
    third = gram_ref[2 * m :]
    low = stack_gram(top[:, :m], top[:, m : 2 * m], top[:, m : 2 * m].T, second[:, m : 2 * m])
    third = jnp.concatenate([third[:, : 2 * m], third[:, 2 * m :]], axis=0)
    high = stack_gram(third[:, :m], third[:, m:], third[:, m:].T, second[:, :m])
    cross = jnp.concatenate([top[:, 2 * m :], second[:, 2 * m :]], axis=0)
    low_mix, high_mix = mixings([low, high], mix)
    gram = stack_gram(
        dot_nt(dot_nn(low_mix, low), low_mix),
        dot_nt(dot_nn(low_mix, cross), high_mix),
        dot_nt(dot_nt(high_mix, cross), low_mix),
        dot_nt(dot_nn(high_mix, high), high_mix),
    )
    last = mixings([gram], mix)[0]
    whole = jnp.concatenate([dot_nn(last[:, :m], low_mix), dot_nn(last[:, m:], high_mix)], axis=1)
    result = joined(bf16_dot(split_two(whole), rows_ref[...]))
    own = m // out_ref.shape[0]
    for i in range(out_ref.shape[0]):
        out_ref[i] = result[i * own : (i + 1) * own].astype(BF16)


VMEM = pl.BlockSpec(memory_space=pltpu.VMEM)
SMEM = pl.BlockSpec(memory_space=pltpu.SMEM)
HBM_SPACE = pltpu.HBM


def call(kernel, out_shape, in_specs, name, flops=0, scratch=()):
    return pl.pallas_call(
        kernel,
        out_shape=out_shape,
        in_specs=in_specs,
        out_specs=jax.tree.map(lambda _: VMEM, out_shape),
        scratch_shapes=scratch,
        compiler_params=pltpu.CompilerParams(vmem_limit_bytes=VMEM_LIMIT),
        cost_estimate=pl.CostEstimate(flops=flops, bytes_accessed=0, transcendentals=0),
        name=name,
    )


def swap(block, axis, mask):
    count = lax.axis_size(axis)
    return lax.ppermute(block, axis, [(i, i ^ mask) for i in range(count)])


def butterfly(block, axis, masks):
    for mask in masks:
        block = block + swap(block, axis, mask)
    return block


EARLY = (1, 4)
LATE = (3, 8, 24)


def shards(snaps, sketch, merge_mix):
    width, points = snaps.shape
    modes = sketch.shape[0]
    snap_count = lax.axis_size("snap")
    chunk = points // snap_count
    chips = snap_count // 2
    position = lax.axis_index("snap")
    place = jnp.stack([position % 2, position // 2]).astype(jnp.int32)
    shape = jax.ShapeDtypeStruct

    own_gram, mine, away = call(
        own_gram_kernel,
        (shape((width, 2 * width), F32),) + (shape((width, chips * chunk), snaps.dtype),) * 2,
        [SMEM, pl.BlockSpec(memory_space=HBM_SPACE)],
        "own_gram",
        scratch=[pltpu.SemaphoreType.DMA((2 * chips,))],
    )(place, snaps)
    other = swap(away, "snap", 1)
    own_gram = butterfly(own_gram, "space", EARLY)

    cross = call(
        cross_gram_kernel,
        shape((width, 2 * width), F32),
        [SMEM] + [VMEM] * 2,
        "cross_gram",
    )(place, mine, other)
    cross = butterfly(cross, "snap", (1,))
    grams = butterfly(own_gram + cross, "space", LATE)
    crossed = butterfly(grams, "space", EARLY)

    work = 4 * 10**9
    half = call(
        functools.partial(power_kernel, ITERS // 2, False),
        shape((modes, width), F32),
        [VMEM] * 2,
        "power_first",
        work,
    )(grams, sketch)
    coeffs = call(
        functools.partial(power_kernel, ITERS - ITERS // 2, True),
        shape((modes, 2 * width), F32),
        [VMEM] * 2,
        "power_last",
        work,
    )(grams, half)
    other_coeffs = swap(coeffs, "snap", 1)

    pieces = call(
        merge_kernel,
        (shape((modes, chunk), BF16),) * chips,
        [SMEM] + [VMEM] * 6,
        "merge",
    )(place, crossed, coeffs, other_coeffs, merge_mix, mine, other)

    pieces = [pieces[0]] + [swap(pieces[i], "snap", 2 * i) for i in range(1, chips)]
    rows, gram = call(
        rows_gram_kernel,
        (shape((chips * modes, chunk), BF16), shape((5 * modes // 2, chips * modes), F32)),
        [SMEM] + [VMEM] * chips,
        "rows_gram",
    )(place, *pieces)
    gram = butterfly(gram, "snap", (1, 2, 6))
    gram = butterfly(gram, "space", EARLY + LATE)

    merged = call(
        tree_kernel,
        shape((snap_count, modes // snap_count, chunk), BF16),
        [VMEM] * 3,
        "tree",
        work,
    )(gram, merge_mix, rows)
    basis = lax.all_to_all(merged, "snap", 0, 0, tiled=True)
    return basis.transpose(1, 0, 2).reshape(modes // snap_count, points).astype(F32)


def solution(mesh):
    in_specs = (P("snap", "space"), P(None, "snap"), P())
    out_specs = P("snap", "space")
    return jax.shard_map(shards, mesh=mesh, in_specs=in_specs, out_specs=out_specs, check_vma=False)
```

```python
import functools
import math

import jax
import jax.numpy as jnp
from jax import lax
from jax.experimental import pallas as pl
from jax.experimental.pallas import tpu as pltpu
from jax.sharding import PartitionSpec as P

ITERS = 4
PANEL = 8
F32 = jnp.float32
BF16 = jnp.bfloat16
VMEM_LIMIT = 24 * 1024 * 1024


def dot_nn(a, b):
    return jnp.dot(a, b, precision=lax.Precision.HIGHEST, preferred_element_type=F32)


def dot_nt(a, b):
    return lax.dot_general(
        a, b, (((1,), (1,)), ((), ())), precision=lax.Precision.HIGHEST, preferred_element_type=F32
    )


def dot_tn(a, b):
    return lax.dot_general(
        a, b, (((0,), (0,)), ((), ())), precision=lax.Precision.HIGHEST, preferred_element_type=F32
    )


def eliminate_panel(table, wide, first):
    group, inner = divmod(first, 8)
    shape = table[0].shape
    row_ids = lax.broadcasted_iota(jnp.int32, shape, 0)
    columns = [
        [jnp.broadcast_to(t[:, wide + first + k : wide + first + k + 1], shape) for t in table[group:]]
        for k in range(PANEL)
    ]
    rows = [jnp.broadcast_to(table[group][inner + k : inner + k + 1], shape) for k in range(PANEL)]
    corner = {
        (k, l): jnp.broadcast_to(columns[k][0][inner + l : inner + l + 1], shape)
        for k in range(PANEL)
        for l in range(k, PANEL)
    }
    for k in range(PANEL):
        inverse = 1.0 / corner[k, k]
        factors = [c * inverse for c in columns[k]]
        steps = {l: corner[k, l] * inverse for l in range(k + 1, PANEL)}
        for l in range(k + 1, PANEL):
            for m in range(l, PANEL):
                corner[l, m] = corner[l, m] - steps[l] * corner[k, m]
            columns[l] = [c - f * corner[k, l] for c, f in zip(columns[l], factors)]
            rows[l] = rows[l] - steps[l] * rows[k]
        factors[0] = jnp.where(row_ids > inner + k, factors[0], 0.0)
        for g, f in enumerate(factors):
            table[group + g] = table[group + g] - f * rows[k]


def cholesky_solves(pairs):
    modes = pairs[0][0].shape[0]
    wide = pairs[0][1].shape[1]
    tables = []
    for h, b in pairs:
        table = jnp.concatenate([b, h], axis=1)
        tables.append([table[r : r + 8] for r in range(0, modes, 8)])
    for first in range(0, modes, PANEL):
        for table in tables:
            eliminate_panel(table, wide, first)
    solved = []
    for table in tables:
        whole = jnp.concatenate(table, axis=0)
        below = whole[:, wide:]
        same = lax.broadcasted_iota(jnp.int32, below.shape, 0) == lax.broadcasted_iota(
            jnp.int32, below.shape, 1
        )
        diagonal = jnp.sum(jnp.where(same, below, 0.0), axis=1, keepdims=True)
        solved.append(whole[:, :wide] * lax.rsqrt(diagonal))
    return solved


def trace_scale(gram):
    same = lax.broadcasted_iota(jnp.int32, gram.shape, 0) == lax.broadcasted_iota(
        jnp.int32, gram.shape, 1
    )
    diagonal = jnp.where(same, gram, 0.0)
    return lax.rsqrt(jnp.sum(jnp.sum(diagonal, axis=1, keepdims=True), axis=0, keepdims=True))


def mixings(grams, mix):
    pairs = []
    for gram in grams:
        curved_t = dot_tn(mix, gram)
        pairs.append((dot_nn(curved_t, mix), curved_t))
    return [s * trace_scale(g) for s, g in zip(cholesky_solves(pairs), grams)]


def split_two(x):
    high = x.astype(BF16)
    return jnp.concatenate([high, (x - high.astype(F32)).astype(BF16)], axis=0)


def bf16_dot(a, b):
    return jnp.dot(a, b, preferred_element_type=F32)


def bf16_dot_nt(a, b):
    return lax.dot_general(a, b, (((1,), (1,)), ((), ())), preferred_element_type=F32)


def joined(both):
    modes = both.shape[0] // 2
    return both[:modes] + both[modes:]


def own_gram_kernel(place_ref, snaps_ref, gram_ref, mine_ref, away_ref, sems):
    core = place_ref[0]
    width, points = mine_ref.shape
    chips = sems.shape[0] // 2
    chunk = points // chips
    parts = []
    for packed_ref, parity in ((mine_ref, core), (away_ref, 1 - core)):
        copies = []
        for i in range(chips):
            there = pl.ds(pl.multiple_of((2 * i + parity) * chunk, chunk), chunk)
            here = pl.ds(i * chunk, chunk)
            sem = sems.at[len(parts) * chips + i]
            copies.append(pltpu.make_async_copy(snaps_ref.at[:, there], packed_ref.at[:, here], sem))
        parts.append((packed_ref, copies))
    for _, copies in parts:
        for copy in copies:
            copy.start()
    grams = []
    for packed_ref, copies in parts:
        for copy in copies:
            copy.wait()
        rows = packed_ref[...]
        grams.append(bf16_dot_nt(rows, rows))
    gram_ref[...] = jnp.zeros_like(gram_ref)
    gram_ref[:, :width] = grams[0] + grams[1]


def cross_gram_kernel(place_ref, mine_ref, other_ref, gram_ref):
    width = mine_ref.shape[0]
    gram_ref[...] = jnp.zeros_like(gram_ref)

    @pl.when(place_ref[0] == 0)
    def _():
        gram_ref[:, width:] = bf16_dot_nt(mine_ref[...], other_ref[...])

    @pl.when(place_ref[0] != 0)
    def _():
        gram_ref[:, width:] = bf16_dot_nt(other_ref[...], mine_ref[...])


def power_kernel(iters, last, gram_ref, coeffs_ref, out_ref):
    coeffs = coeffs_ref[...].astype(F32)
    width = coeffs.shape[1]
    modes = coeffs.shape[0]
    gram = gram_ref[:, :width]
    scale = 1.0 / math.sqrt(width)
    for _ in range(iters):
        weighted = dot_nn(coeffs, gram)
        solved = cholesky_solves([(dot_nt(weighted, coeffs), weighted)])[0]
        coeffs = solved.astype(BF16).astype(F32) * scale
    if last:
        out_ref[...] = jnp.zeros_like(out_ref)
        out_ref[:, :width] = coeffs
        out_ref[:, width : width + modes] = dot_nt(dot_nn(coeffs, gram), coeffs)
    else:
        out_ref[...] = coeffs


def stack_gram(low, cross, cross_t, high):
    return jnp.concatenate(
        [jnp.concatenate([low, cross], axis=1), jnp.concatenate([cross_t, high], axis=1)], axis=0
    )


def merge_kernel(place_ref, cross_ref, mine_co_ref, other_co_ref, mix_ref, mine_ref, other_ref, *out_refs):
    first = place_ref[0] == 0
    width = mine_ref.shape[0]
    modes = mine_co_ref.shape[0]
    mine_co, other_co = mine_co_ref[...], other_co_ref[...]
    low = jnp.where(first, mine_co, other_co)
    high = jnp.where(first, other_co, mine_co)
    low_co, high_co = low[:, :width], high[:, :width]
    cross = cross_ref[:, width:]
    gram = stack_gram(
        low[:, width : width + modes],
        dot_nt(dot_nn(low_co, cross), high_co),
        dot_nt(dot_nt(high_co, cross), low_co),
        high[:, width : width + modes],
    )
    mixing = mixings([gram], mix_ref[...])[0]
    low_mix = dot_nn(mixing[:, :modes], low_co)
    high_mix = dot_nn(mixing[:, modes:], high_co)
    mine_split = split_two(jnp.where(first, low_mix, high_mix))
    other_split = split_two(jnp.where(first, high_mix, low_mix))
    chips = (len(out_refs) + 1) // 2
    piece_refs, rest_refs = out_refs[:chips], out_refs[chips:]
    chunk = piece_refs[0].shape[1]
    split = jnp.concatenate([mine_split, other_split], axis=1)
    for i in range(chips):
        here = pl.ds(pl.multiple_of((place_ref[1] ^ i) * chunk, chunk), chunk)
        rows = jnp.concatenate([mine_ref[:, here], other_ref[:, here]], axis=0)
        piece = joined(bf16_dot(split, rows)).astype(BF16)
        piece_refs[i][...] = piece
        for apart in range(1, chips):
            if apart != i:
                at = rest_place(apart, i) * modes
                rest_refs[apart - 1][at : at + modes] = piece


def rest_place(apart, i):
    return i if i < apart else i - 1


def rows_gram_kernel(place_ref, *refs):
    piece_refs, (gram_ref, rows_ref) = refs[:-2], refs[-2:]
    modes = piece_refs[0].shape[0]
    for i, piece_ref in enumerate(piece_refs):
        start = pl.multiple_of((place_ref[1] ^ i) * modes, modes)
        rows_ref[pl.ds(start, modes), :] = piece_ref[...]
    rows = rows_ref[...]
    gram = bf16_dot_nt(rows, rows)
    m, h = modes, modes // 2
    gram_ref[:m] = gram[:m]
    gram_ref[m : 2 * m] = gram[m : 2 * m]
    gram_ref[m : 2 * m, :m] = gram[3 * m :, 3 * m :]
    gram_ref[2 * m :, : 2 * m] = gram[2 * m : 2 * m + h, 2 * m :]
    gram_ref[2 * m :, 2 * m :] = gram[2 * m + h : 3 * m, 2 * m :]


def tree_kernel(gram_ref, mix_ref, whole_ref):
    mix = mix_ref[...]
    m = mix.shape[1]
    h = m // 2
    top = gram_ref[:m]
    second = gram_ref[m : 2 * m]
    third = gram_ref[2 * m :]
    low = stack_gram(top[:, :m], top[:, m : 2 * m], top[:, m : 2 * m].T, second[:, m : 2 * m])
    third = jnp.concatenate([third[:, : 2 * m], third[:, 2 * m :]], axis=0)
    high = stack_gram(third[:, :m], third[:, m:], third[:, m:].T, second[:, :m])
    cross = jnp.concatenate([top[:, 2 * m :], second[:, 2 * m :]], axis=0)
    low_mix, high_mix = mixings([low, high], mix)
    gram = stack_gram(
        dot_nt(dot_nn(low_mix, low), low_mix),
        dot_nt(dot_nn(low_mix, cross), high_mix),
        dot_nt(dot_nt(high_mix, cross), low_mix),
        dot_nt(dot_nn(high_mix, high), high_mix),
    )
    last = mixings([gram], mix)[0]
    whole_ref[...] = jnp.concatenate(
        [dot_nn(last[:, :m], low_mix), dot_nn(last[:, m:], high_mix)], axis=1
    )


def finish_kernel(place_ref, whole_ref, *refs):
    keep_ref, give_ref = refs[-2:]
    chips = (len(refs) + 1) // 3
    own_refs, got_refs, rest_refs = refs[:chips], refs[chips : 2 * chips - 1], refs[2 * chips - 1 : -2]
    core, chip = place_ref[0], place_ref[1]
    modes, chunk = own_refs[0].shape
    own = 2 * keep_ref.shape[0]
    mixing = whole_ref[pl.ds(pl.multiple_of(chip * own, own), own), :]
    mixing = jnp.where(chip & 2 != 0, pltpu.roll(mixing, 2 * modes, 1), mixing)
    lanes = lax.broadcasted_iota(jnp.int32, mixing.shape, 1)
    turned = jnp.where(
        (lanes // modes) % 2 == 0,
        pltpu.roll(mixing, (chips - 1) * modes, 1),
        pltpu.roll(mixing, modes, 1),
    )
    split = split_two(jnp.where(chip & 1 != 0, turned, mixing))
    for r in range(chips):
        blocks = [own_refs[r][...]]
        for apart in range(1, chips):
            if r == 0:
                blocks.append(got_refs[apart - 1][...])
            else:
                at = rest_place(apart, apart ^ r) * modes
                blocks.append(rest_refs[apart - 1][at : at + modes])
        part = joined(bf16_dot(split, jnp.concatenate(blocks, axis=0)))
        low, high = part[: own // 2], part[own // 2 :]
        there = pl.ds(pl.multiple_of((chip ^ r) * chunk, chunk), chunk)
        keep_ref[:, there] = jnp.where(core == 0, low, high)
        give_ref[:, there] = jnp.where(core == 0, high, low)


def assemble_kernel(place_ref, keep_ref, got_ref, out_ref):
    core = place_ref[0]
    chips = out_ref.shape[1] // keep_ref.shape[1] * 2
    chunk = keep_ref.shape[1] // chips
    for i in range(chips):
        here = pl.ds(i * chunk, chunk)
        out_ref[:, pl.ds(pl.multiple_of((2 * i + core) * chunk, chunk), chunk)] = keep_ref[:, here]
        out_ref[:, pl.ds(pl.multiple_of((2 * i + 1 - core) * chunk, chunk), chunk)] = got_ref[:, here]


VMEM = pl.BlockSpec(memory_space=pltpu.VMEM)
SMEM = pl.BlockSpec(memory_space=pltpu.SMEM)
HBM_SPACE = pltpu.HBM


def call(kernel, out_shape, in_specs, name, flops=0, scratch=()):
    return pl.pallas_call(
        kernel,
        out_shape=out_shape,
        in_specs=in_specs,
        out_specs=jax.tree.map(lambda _: VMEM, out_shape),
        scratch_shapes=scratch,
        compiler_params=pltpu.CompilerParams(vmem_limit_bytes=VMEM_LIMIT),
        cost_estimate=pl.CostEstimate(flops=flops, bytes_accessed=0, transcendentals=0),
        name=name,
    )


def swap(block, axis, mask):
    count = lax.axis_size(axis)
    return lax.ppermute(block, axis, [(i, i ^ mask) for i in range(count)])


def butterfly(block, axis, masks):
    for mask in masks:
        block = block + swap(block, axis, mask)
    return block


EARLY = (1, 4)
LATE = (3, 8, 24)


def shards(snaps, sketch, merge_mix):
    width, points = snaps.shape
    modes = sketch.shape[0]
    snap_count = lax.axis_size("snap")
    chunk = points // snap_count
    chips = snap_count // 2
    position = lax.axis_index("snap")
    place = jnp.stack([position % 2, position // 2]).astype(jnp.int32)
    shape = jax.ShapeDtypeStruct

    own_gram, mine, away = call(
        own_gram_kernel,
        (shape((width, 2 * width), F32),) + (shape((width, chips * chunk), snaps.dtype),) * 2,
        [SMEM, pl.BlockSpec(memory_space=HBM_SPACE)],
        "own_gram",
        scratch=[pltpu.SemaphoreType.DMA((2 * chips,))],
    )(place, snaps)
    other = swap(away, "snap", 1)
    own_gram = butterfly(own_gram, "space", EARLY)

    cross = call(
        cross_gram_kernel,
        shape((width, 2 * width), F32),
        [SMEM] + [VMEM] * 2,
        "cross_gram",
    )(place, mine, other)
    cross = butterfly(cross, "snap", (1,))
    grams = butterfly(own_gram + cross, "space", LATE)
    crossed = butterfly(grams, "space", EARLY)

    work = 4 * 10**9
    half = call(
        functools.partial(power_kernel, ITERS // 2, False),
        shape((modes, width), F32),
        [VMEM] * 2,
        "power_first",
        work,
    )(grams, sketch)
    coeffs = call(
        functools.partial(power_kernel, ITERS - ITERS // 2, True),
        shape((modes, 2 * width), F32),
        [VMEM] * 2,
        "power_last",
        work,
    )(grams, half)
    other_coeffs = swap(coeffs, "snap", 1)

    sent = call(
        merge_kernel,
        (shape((modes, chunk), BF16),) * chips + (shape(((chips - 1) * modes, chunk), BF16),) * (chips - 1),
        [SMEM] + [VMEM] * 6,
        "merge",
    )(place, crossed, coeffs, other_coeffs, merge_mix, mine, other)
    pieces, rests = sent[:chips], sent[chips:]

    got = [swap(pieces[i], "snap", 2 * i) for i in range(1, chips)]
    rests, got = lax.optimization_barrier((tuple(rests), tuple(got)))
    rests = [swap(rest, "snap", 2 * i) for i, rest in enumerate(rests, 1)]
    gram = call(
        rows_gram_kernel,
        shape((5 * modes // 2, chips * modes), F32),
        [SMEM] + [VMEM] * chips,
        "rows_gram",
        scratch=[pltpu.VMEM((chips * modes, chunk), BF16)],
    )(place, pieces[0], *got)
    gram = butterfly(gram, "snap", (1,))
    gram = butterfly(gram, "space", EARLY + LATE)
    gram = butterfly(gram, "snap", (2, 6))

    whole = call(
        tree_kernel, shape((modes, chips * modes), F32), [VMEM] * 2, "tree", work
    )(gram, merge_mix)
    half_out = shape((modes // snap_count, points // 2), F32)
    keep, give = call(
        finish_kernel,
        (half_out, half_out),
        [SMEM] + [VMEM] * (3 * chips - 1),
        "finish",
    )(place, whole, *pieces, *got, *rests)
    return call(
        assemble_kernel,
        shape((modes // snap_count, points), F32),
        [SMEM] + [VMEM] * 2,
        "assemble",
    )(place, keep, swap(give, "snap", 1))


def solution(mesh):
    in_specs = (P("snap", "space"), P(None, "snap"), P())
    out_specs = P("snap", "space")
    return jax.shard_map(shards, mesh=mesh, in_specs=in_specs, out_specs=out_specs, check_vma=False)
```

```python
import functools
import math

import jax
import jax.numpy as jnp
from jax import lax
from jax.experimental import pallas as pl
from jax.experimental.pallas import tpu as pltpu
from jax.sharding import PartitionSpec as P

ITERS = 4
PANEL = 8
F32 = jnp.float32
BF16 = jnp.bfloat16
VMEM_LIMIT = 24 * 1024 * 1024


def dot_nn(a, b):
    return jnp.dot(a, b, precision=lax.Precision.HIGHEST, preferred_element_type=F32)


def dot_nt(a, b):
    return lax.dot_general(
        a, b, (((1,), (1,)), ((), ())), precision=lax.Precision.HIGHEST, preferred_element_type=F32
    )


def dot_tn(a, b):
    return lax.dot_general(
        a, b, (((0,), (0,)), ((), ())), precision=lax.Precision.HIGHEST, preferred_element_type=F32
    )


def eliminate_panel(table, wide, first):
    group, inner = divmod(first, 8)
    shape = table[0].shape
    row_ids = lax.broadcasted_iota(jnp.int32, shape, 0)
    columns = [
        [jnp.broadcast_to(t[:, wide + first + k : wide + first + k + 1], shape) for t in table[group:]]
        for k in range(PANEL)
    ]
    rows = [jnp.broadcast_to(table[group][inner + k : inner + k + 1], shape) for k in range(PANEL)]
    corner = {
        (k, l): jnp.broadcast_to(columns[k][0][inner + l : inner + l + 1], shape)
        for k in range(PANEL)
        for l in range(k, PANEL)
    }
    for k in range(PANEL):
        inverse = 1.0 / corner[k, k]
        factors = [c * inverse for c in columns[k]]
        steps = {l: corner[k, l] * inverse for l in range(k + 1, PANEL)}
        for l in range(k + 1, PANEL):
            for m in range(l, PANEL):
                corner[l, m] = corner[l, m] - steps[l] * corner[k, m]
            columns[l] = [c - f * corner[k, l] for c, f in zip(columns[l], factors)]
            rows[l] = rows[l] - steps[l] * rows[k]
        factors[0] = jnp.where(row_ids > inner + k, factors[0], 0.0)
        for g, f in enumerate(factors):
            table[group + g] = table[group + g] - f * rows[k]


def cholesky_solves(pairs):
    modes = pairs[0][0].shape[0]
    wide = pairs[0][1].shape[1]
    tables = []
    for h, b in pairs:
        table = jnp.concatenate([b, h], axis=1)
        tables.append([table[r : r + 8] for r in range(0, modes, 8)])
    for first in range(0, modes, PANEL):
        for table in tables:
            eliminate_panel(table, wide, first)
    solved = []
    for table in tables:
        whole = jnp.concatenate(table, axis=0)
        below = whole[:, wide:]
        same = lax.broadcasted_iota(jnp.int32, below.shape, 0) == lax.broadcasted_iota(
            jnp.int32, below.shape, 1
        )
        diagonal = jnp.sum(jnp.where(same, below, 0.0), axis=1, keepdims=True)
        solved.append(whole[:, :wide] * lax.rsqrt(diagonal))
    return solved


def trace_scale(gram):
    same = lax.broadcasted_iota(jnp.int32, gram.shape, 0) == lax.broadcasted_iota(
        jnp.int32, gram.shape, 1
    )
    diagonal = jnp.where(same, gram, 0.0)
    return lax.rsqrt(jnp.sum(jnp.sum(diagonal, axis=1, keepdims=True), axis=0, keepdims=True))


def mixings(grams, mix):
    pairs = []
    for gram in grams:
        curved_t = dot_tn(mix, gram)
        pairs.append((dot_nn(curved_t, mix), curved_t))
    return [s * trace_scale(g) for s, g in zip(cholesky_solves(pairs), grams)]


def split_two(x):
    high = x.astype(BF16)
    return jnp.concatenate([high, (x - high.astype(F32)).astype(BF16)], axis=0)


def bf16_dot(a, b):
    return jnp.dot(a, b, preferred_element_type=F32)


def bf16_dot_nt(a, b):
    return lax.dot_general(a, b, (((1,), (1,)), ((), ())), preferred_element_type=F32)


def joined(both):
    modes = both.shape[0] // 2
    return both[:modes] + both[modes:]


def own_gram_kernel(place_ref, snaps_ref, gram_ref, mine_ref, away_ref, sems):
    core = place_ref[0]
    width, points = mine_ref.shape
    chips = sems.shape[0] // 2
    chunk = points // chips
    parts = []
    for packed_ref, parity in ((mine_ref, core), (away_ref, 1 - core)):
        copies = []
        for i in range(chips):
            there = pl.ds(pl.multiple_of((2 * i + parity) * chunk, chunk), chunk)
            here = pl.ds(i * chunk, chunk)
            sem = sems.at[len(parts) * chips + i]
            copies.append(pltpu.make_async_copy(snaps_ref.at[:, there], packed_ref.at[:, here], sem))
        parts.append((packed_ref, copies))
    for _, copies in parts:
        for copy in copies:
            copy.start()
    grams = []
    for packed_ref, copies in parts:
        for copy in copies:
            copy.wait()
        rows = packed_ref[...]
        grams.append(bf16_dot_nt(rows, rows))
    gram_ref[...] = jnp.zeros_like(gram_ref)
    gram_ref[:, :width] = grams[0] + grams[1]


def cross_gram_kernel(place_ref, mine_ref, other_ref, gram_ref):
    width = mine_ref.shape[0]
    gram_ref[...] = jnp.zeros_like(gram_ref)

    @pl.when(place_ref[0] == 0)
    def _():
        gram_ref[:, width:] = bf16_dot_nt(mine_ref[...], other_ref[...])

    @pl.when(place_ref[0] != 0)
    def _():
        gram_ref[:, width:] = bf16_dot_nt(other_ref[...], mine_ref[...])


def power_kernel(iters, last, gram_ref, coeffs_ref, out_ref):
    coeffs = coeffs_ref[...].astype(F32)
    width = coeffs.shape[1]
    modes = coeffs.shape[0]
    gram = gram_ref[:, :width]
    scale = 1.0 / math.sqrt(width)
    for _ in range(iters):
        weighted = dot_nn(coeffs, gram)
        solved = cholesky_solves([(dot_nt(weighted, coeffs), weighted)])[0]
        coeffs = solved.astype(BF16).astype(F32) * scale
    if last:
        out_ref[...] = jnp.zeros_like(out_ref)
        out_ref[:, :width] = coeffs
        out_ref[:, width : width + modes] = dot_nt(dot_nn(coeffs, gram), coeffs)
    else:
        out_ref[...] = coeffs


def stack_gram(low, cross, cross_t, high):
    return jnp.concatenate(
        [jnp.concatenate([low, cross], axis=1), jnp.concatenate([cross_t, high], axis=1)], axis=0
    )


def merge_kernel(place_ref, cross_ref, mine_co_ref, other_co_ref, mix_ref, mine_ref, other_hbm, *refs):
    out_refs, (other_ref, sem) = refs[:-2], refs[-2:]
    fetch = pltpu.make_async_copy(other_hbm, other_ref, sem)
    fetch.start()
    first = place_ref[0] == 0
    width = mine_ref.shape[0]
    modes = mine_co_ref.shape[0]
    mine_co, other_co = mine_co_ref[...], other_co_ref[...]
    low = jnp.where(first, mine_co, other_co)
    high = jnp.where(first, other_co, mine_co)
    low_co, high_co = low[:, :width], high[:, :width]
    cross = cross_ref[:, width:]
    gram = stack_gram(
        low[:, width : width + modes],
        dot_nt(dot_nn(low_co, cross), high_co),
        dot_nt(dot_nt(high_co, cross), low_co),
        high[:, width : width + modes],
    )
    mixing = mixings([gram], mix_ref[...])[0]
    low_mix = dot_nn(mixing[:, :modes], low_co)
    high_mix = dot_nn(mixing[:, modes:], high_co)
    mine_split = split_two(jnp.where(first, low_mix, high_mix))
    other_split = split_two(jnp.where(first, high_mix, low_mix))
    chips = (len(out_refs) + 1) // 2
    piece_refs, rest_refs = out_refs[:chips], out_refs[chips:]
    chunk = piece_refs[0].shape[1]
    split = jnp.concatenate([mine_split, other_split], axis=1)
    fetch.wait()
    for i in range(chips):
        here = pl.ds(pl.multiple_of((place_ref[1] ^ i) * chunk, chunk), chunk)
        rows = jnp.concatenate([mine_ref[:, here], other_ref[:, here]], axis=0)
        piece = joined(bf16_dot(split, rows)).astype(BF16)
        piece_refs[i][...] = piece
        for apart in range(1, chips):
            if apart != i:
                at = rest_place(apart, i) * modes
                rest_refs[apart - 1][at : at + modes] = piece


def rest_place(apart, i):
    return i if i < apart else i - 1


def rows_gram_kernel(place_ref, *refs):
    piece_refs, (gram_ref, rows_ref) = refs[:-2], refs[-2:]
    modes = piece_refs[0].shape[0]
    for i, piece_ref in enumerate(piece_refs):
        start = pl.multiple_of((place_ref[1] ^ i) * modes, modes)
        rows_ref[pl.ds(start, modes), :] = piece_ref[...]
    rows = rows_ref[...]
    gram = bf16_dot_nt(rows, rows)
    m, h = modes, modes // 2
    gram_ref[:m] = gram[:m]
    gram_ref[m : 2 * m] = gram[m : 2 * m]
    gram_ref[m : 2 * m, :m] = gram[3 * m :, 3 * m :]
    gram_ref[2 * m :, : 2 * m] = gram[2 * m : 2 * m + h, 2 * m :]
    gram_ref[2 * m :, 2 * m :] = gram[2 * m + h : 3 * m, 2 * m :]


def tree_kernel(gram_ref, mix_ref, whole_ref):
    mix = mix_ref[...]
    m = mix.shape[1]
    h = m // 2
    top = gram_ref[:m]
    second = gram_ref[m : 2 * m]
    third = gram_ref[2 * m :]
    low = stack_gram(top[:, :m], top[:, m : 2 * m], top[:, m : 2 * m].T, second[:, m : 2 * m])
    third = jnp.concatenate([third[:, : 2 * m], third[:, 2 * m :]], axis=0)
    high = stack_gram(third[:, :m], third[:, m:], third[:, m:].T, second[:, :m])
    cross = jnp.concatenate([top[:, 2 * m :], second[:, 2 * m :]], axis=0)
    low_mix, high_mix = mixings([low, high], mix)
    gram = stack_gram(
        dot_nt(dot_nn(low_mix, low), low_mix),
        dot_nt(dot_nn(low_mix, cross), high_mix),
        dot_nt(dot_nt(high_mix, cross), low_mix),
        dot_nt(dot_nn(high_mix, high), high_mix),
    )
    last = mixings([gram], mix)[0]
    whole_ref[...] = jnp.concatenate(
        [dot_nn(last[:, :m], low_mix), dot_nn(last[:, m:], high_mix)], axis=1
    )


def finish_kernel(place_ref, whole_ref, *refs):
    keep_ref, give_ref = refs[-2:]
    chips = (len(refs) + 1) // 3
    own_refs, got_refs, rest_refs = refs[:chips], refs[chips : 2 * chips - 1], refs[2 * chips - 1 : -2]
    core, chip = place_ref[0], place_ref[1]
    modes, chunk = own_refs[0].shape
    own = 2 * keep_ref.shape[0]
    mixing = whole_ref[pl.ds(pl.multiple_of(chip * own, own), own), :]
    mixing = jnp.where(chip & 2 != 0, pltpu.roll(mixing, 2 * modes, 1), mixing)
    lanes = lax.broadcasted_iota(jnp.int32, mixing.shape, 1)
    turned = jnp.where(
        (lanes // modes) % 2 == 0,
        pltpu.roll(mixing, (chips - 1) * modes, 1),
        pltpu.roll(mixing, modes, 1),
    )
    split = split_two(jnp.where(chip & 1 != 0, turned, mixing))
    for r in range(chips):
        blocks = [own_refs[r][...]]
        for apart in range(1, chips):
            if r == 0:
                blocks.append(got_refs[apart - 1][...])
            else:
                at = rest_place(apart, apart ^ r) * modes
                blocks.append(rest_refs[apart - 1][at : at + modes])
        part = joined(bf16_dot(split, jnp.concatenate(blocks, axis=0)))
        low, high = part[: own // 2], part[own // 2 :]
        there = pl.ds(pl.multiple_of((chip ^ r) * chunk, chunk), chunk)
        keep_ref[:, there] = jnp.where(core == 0, low, high)
        give_ref[:, there] = jnp.where(core == 0, high, low)


def assemble_kernel(place_ref, keep_ref, got_ref, out_ref):
    core = place_ref[0]
    chips = out_ref.shape[1] // keep_ref.shape[1] * 2
    chunk = keep_ref.shape[1] // chips
    for i in range(chips):
        here = pl.ds(i * chunk, chunk)
        out_ref[:, pl.ds(pl.multiple_of((2 * i + core) * chunk, chunk), chunk)] = keep_ref[:, here]
        out_ref[:, pl.ds(pl.multiple_of((2 * i + 1 - core) * chunk, chunk), chunk)] = got_ref[:, here]


VMEM = pl.BlockSpec(memory_space=pltpu.VMEM)
SMEM = pl.BlockSpec(memory_space=pltpu.SMEM)
HBM_SPACE = pltpu.HBM


def call(kernel, out_shape, in_specs, name, flops=0, scratch=(), vmem=VMEM_LIMIT):
    return pl.pallas_call(
        kernel,
        out_shape=out_shape,
        in_specs=in_specs,
        out_specs=jax.tree.map(lambda _: VMEM, out_shape),
        scratch_shapes=scratch,
        compiler_params=pltpu.CompilerParams(vmem_limit_bytes=vmem),
        cost_estimate=pl.CostEstimate(flops=flops, bytes_accessed=0, transcendentals=0),
        name=name,
    )


def swap(block, axis, mask):
    count = lax.axis_size(axis)
    return lax.ppermute(block, axis, [(i, i ^ mask) for i in range(count)])


def butterfly(block, axis, masks):
    for mask in masks:
        block = block + swap(block, axis, mask)
    return block


EARLY = (1, 4)
LATE = (3, 8, 24)


def shards(snaps, sketch, merge_mix):
    width, points = snaps.shape
    modes = sketch.shape[0]
    snap_count = lax.axis_size("snap")
    chunk = points // snap_count
    chips = snap_count // 2
    position = lax.axis_index("snap")
    place = jnp.stack([position % 2, position // 2]).astype(jnp.int32)
    shape = jax.ShapeDtypeStruct

    own_gram, mine, away = call(
        own_gram_kernel,
        (shape((width, 2 * width), F32),) + (shape((width, chips * chunk), snaps.dtype),) * 2,
        [SMEM, pl.BlockSpec(memory_space=HBM_SPACE)],
        "own_gram",
        scratch=[pltpu.SemaphoreType.DMA((2 * chips,))],
        vmem=2 * VMEM_LIMIT,
    )(place, snaps)
    other = swap(away, "snap", 1)
    own_gram = butterfly(own_gram, "space", EARLY)

    cross = call(
        cross_gram_kernel,
        shape((width, 2 * width), F32),
        [SMEM] + [VMEM] * 2,
        "cross_gram",
    )(place, mine, other)
    cross = butterfly(cross, "snap", (1,))
    grams = butterfly(own_gram + cross, "space", LATE)
    crossed = butterfly(grams, "space", EARLY)

    work = 4 * 10**9
    half = call(
        functools.partial(power_kernel, ITERS // 2, False),
        shape((modes, width), F32),
        [VMEM] * 2,
        "power_first",
        work,
    )(grams, sketch)
    coeffs = call(
        functools.partial(power_kernel, ITERS - ITERS // 2, True),
        shape((modes, 2 * width), F32),
        [VMEM] * 2,
        "power_last",
        work,
    )(grams, half)
    other_coeffs = swap(coeffs, "snap", 1)

    sent = call(
        merge_kernel,
        (shape((modes, chunk), BF16),) * chips + (shape(((chips - 1) * modes, chunk), BF16),) * (chips - 1),
        [SMEM] + [VMEM] * 5 + [pl.BlockSpec(memory_space=HBM_SPACE)],
        "merge",
        scratch=[pltpu.VMEM(other.shape, BF16), pltpu.SemaphoreType.DMA],
        vmem=2 * VMEM_LIMIT,
    )(place, crossed, coeffs, other_coeffs, merge_mix, mine, other)
    pieces, rests = sent[:chips], sent[chips:]

    got = [swap(pieces[i], "snap", 2 * i) for i in range(1, chips)]
    gram = call(
        rows_gram_kernel,
        shape((5 * modes // 2, chips * modes), F32),
        [SMEM] + [VMEM] * chips,
        "rows_gram",
        scratch=[pltpu.VMEM((chips * modes, chunk), BF16)],
    )(place, pieces[0], *got)
    gram = butterfly(gram, "snap", (1,))
    moved = []
    for i, (rest, mask) in enumerate(zip(rests, EARLY + LATE), 1):
        gram, rest = lax.optimization_barrier((gram, rest))
        moved.append(swap(rest, "snap", 2 * i))
        gram = butterfly(gram, "space", (mask,))
    gram = butterfly(gram, "space", (EARLY + LATE)[len(rests) :])
    gram = butterfly(gram, "snap", (2, 6))

    whole = call(
        tree_kernel, shape((modes, chips * modes), F32), [VMEM] * 2, "tree", work
    )(gram, merge_mix)
    half_out = shape((modes // snap_count, points // 2), F32)
    keep, give = call(
        finish_kernel,
        (half_out, half_out),
        [SMEM] + [VMEM] * (3 * chips - 1),
        "finish",
    )(place, whole, *pieces, *got, *moved)
    return call(
        assemble_kernel,
        shape((modes // snap_count, points), F32),
        [SMEM] + [VMEM] * 2,
        "assemble",
    )(place, keep, swap(give, "snap", 1))


def solution(mesh):
    in_specs = (P("snap", "space"), P(None, "snap"), P())
    out_specs = P("snap", "space")
    return jax.shard_map(shards, mesh=mesh, in_specs=in_specs, out_specs=out_specs, check_vma=False)
```

```python
import functools
import math

import jax
import jax.numpy as jnp
from jax import lax
from jax.experimental import pallas as pl
from jax.experimental.pallas import tpu as pltpu
from jax.sharding import PartitionSpec as P

ITERS = 4
PANEL = 8
F32 = jnp.float32
BF16 = jnp.bfloat16
VMEM_LIMIT = 24 * 1024 * 1024


def dot_nn(a, b):
    return jnp.dot(a, b, precision=lax.Precision.HIGHEST, preferred_element_type=F32)


def dot_nt(a, b):
    return lax.dot_general(
        a, b, (((1,), (1,)), ((), ())), precision=lax.Precision.HIGHEST, preferred_element_type=F32
    )


def dot_tn(a, b):
    return lax.dot_general(
        a, b, (((0,), (0,)), ((), ())), precision=lax.Precision.HIGHEST, preferred_element_type=F32
    )


def eliminate_panel(table, wide, first):
    group, inner = divmod(first, 8)
    shape = table[0].shape
    row_ids = lax.broadcasted_iota(jnp.int32, shape, 0)
    columns = [
        [jnp.broadcast_to(t[:, wide + first + k : wide + first + k + 1], shape) for t in table[group:]]
        for k in range(PANEL)
    ]
    rows = [jnp.broadcast_to(table[group][inner + k : inner + k + 1], shape) for k in range(PANEL)]
    corner = {
        (k, l): jnp.broadcast_to(columns[k][0][inner + l : inner + l + 1], shape)
        for k in range(PANEL)
        for l in range(k, PANEL)
    }
    for k in range(PANEL):
        inverse = 1.0 / corner[k, k]
        factors = [c * inverse for c in columns[k]]
        steps = {l: corner[k, l] * inverse for l in range(k + 1, PANEL)}
        for l in range(k + 1, PANEL):
            for m in range(l, PANEL):
                corner[l, m] = corner[l, m] - steps[l] * corner[k, m]
            columns[l] = [c - f * corner[k, l] for c, f in zip(columns[l], factors)]
            rows[l] = rows[l] - steps[l] * rows[k]
        factors[0] = jnp.where(row_ids > inner + k, factors[0], 0.0)
        for g, f in enumerate(factors):
            table[group + g] = table[group + g] - f * rows[k]


def cholesky_solves(pairs):
    modes = pairs[0][0].shape[0]
    wide = pairs[0][1].shape[1]
    tables = []
    for h, b in pairs:
        table = jnp.concatenate([b, h], axis=1)
        tables.append([table[r : r + 8] for r in range(0, modes, 8)])
    for first in range(0, modes, PANEL):
        for table in tables:
            eliminate_panel(table, wide, first)
    solved = []
    for table in tables:
        whole = jnp.concatenate(table, axis=0)
        below = whole[:, wide:]
        same = lax.broadcasted_iota(jnp.int32, below.shape, 0) == lax.broadcasted_iota(
            jnp.int32, below.shape, 1
        )
        diagonal = jnp.sum(jnp.where(same, below, 0.0), axis=1, keepdims=True)
        solved.append(whole[:, :wide] * lax.rsqrt(diagonal))
    return solved


def trace_scale(gram):
    same = lax.broadcasted_iota(jnp.int32, gram.shape, 0) == lax.broadcasted_iota(
        jnp.int32, gram.shape, 1
    )
    diagonal = jnp.where(same, gram, 0.0)
    return lax.rsqrt(jnp.sum(jnp.sum(diagonal, axis=1, keepdims=True), axis=0, keepdims=True))


def mixings(grams, mix):
    pairs = []
    for gram in grams:
        curved_t = dot_tn(mix, gram)
        pairs.append((dot_nn(curved_t, mix), curved_t))
    return [s * trace_scale(g) for s, g in zip(cholesky_solves(pairs), grams)]


def split_two(x):
    high = x.astype(BF16)
    return jnp.concatenate([high, (x - high.astype(F32)).astype(BF16)], axis=0)


def bf16_dot(a, b):
    return jnp.dot(a, b, preferred_element_type=F32)


def bf16_dot_nt(a, b):
    return lax.dot_general(a, b, (((1,), (1,)), ((), ())), preferred_element_type=F32)


def joined(both):
    modes = both.shape[0] // 2
    return both[:modes] + both[modes:]


def own_gram_kernel(place_ref, snaps_ref, gram_ref, mine_ref, away_ref, sems):
    core = place_ref[0]
    width, points = mine_ref.shape
    chips = sems.shape[0] // 2
    chunk = points // chips
    parts = []
    for packed_ref, parity in ((mine_ref, core), (away_ref, 1 - core)):
        copies = []
        for i in range(chips):
            there = pl.ds(pl.multiple_of((2 * i + parity) * chunk, chunk), chunk)
            here = pl.ds(i * chunk, chunk)
            sem = sems.at[len(parts) * chips + i]
            copies.append(pltpu.make_async_copy(snaps_ref.at[:, there], packed_ref.at[:, here], sem))
        parts.append((packed_ref, copies))
    for _, copies in parts:
        for copy in copies:
            copy.start()
    grams = []
    for packed_ref, copies in parts:
        for copy in copies:
            copy.wait()
        rows = packed_ref[...]
        grams.append(bf16_dot_nt(rows, rows))
    gram_ref[...] = jnp.zeros_like(gram_ref)
    gram_ref[:, :width] = grams[0] + grams[1]


def cross_gram_kernel(place_ref, mine_ref, other_ref, gram_ref):
    width = mine_ref.shape[0]
    gram_ref[...] = jnp.zeros_like(gram_ref)

    @pl.when(place_ref[0] == 0)
    def _():
        gram_ref[:, width:] = bf16_dot_nt(mine_ref[...], other_ref[...])

    @pl.when(place_ref[0] != 0)
    def _():
        gram_ref[:, width:] = bf16_dot_nt(other_ref[...], mine_ref[...])


def power_kernel(iters, last, gram_ref, coeffs_ref, out_ref):
    coeffs = coeffs_ref[...].astype(F32)
    width = coeffs.shape[1]
    modes = coeffs.shape[0]
    gram = gram_ref[:, :width]
    scale = 1.0 / math.sqrt(width)
    for _ in range(iters):
        weighted = dot_nn(coeffs, gram)
        solved = cholesky_solves([(dot_nt(weighted, coeffs), weighted)])[0]
        coeffs = solved.astype(BF16).astype(F32) * scale
    if last:
        out_ref[...] = jnp.zeros_like(out_ref)
        out_ref[:, :width] = coeffs
        out_ref[:, width : width + modes] = dot_nt(dot_nn(coeffs, gram), coeffs)
    else:
        out_ref[...] = coeffs


def stack_gram(low, cross, cross_t, high):
    return jnp.concatenate(
        [jnp.concatenate([low, cross], axis=1), jnp.concatenate([cross_t, high], axis=1)], axis=0
    )


def merge_kernel(place_ref, cross_ref, mine_co_ref, other_co_ref, mix_ref, mine_ref, other_hbm, *refs):
    out_refs, (other_ref, sem) = refs[:-2], refs[-2:]
    parts = sem.shape[0]
    part = other_ref.shape[0] // parts
    fetches = [
        pltpu.make_async_copy(other_hbm.at[pl.ds(i * part, part)], other_ref.at[pl.ds(i * part, part)], sem.at[i])
        for i in range(parts)
    ]
    for fetch in fetches:
        fetch.start()
    first = place_ref[0] == 0
    width = mine_ref.shape[0]
    modes = mine_co_ref.shape[0]
    mine_co, other_co = mine_co_ref[...], other_co_ref[...]
    low = jnp.where(first, mine_co, other_co)
    high = jnp.where(first, other_co, mine_co)
    low_co, high_co = low[:, :width], high[:, :width]
    cross = cross_ref[:, width:]
    gram = stack_gram(
        low[:, width : width + modes],
        dot_nt(dot_nn(low_co, cross), high_co),
        dot_nt(dot_nt(high_co, cross), low_co),
        high[:, width : width + modes],
    )
    mixing = mixings([gram], mix_ref[...])[0]
    low_mix = dot_nn(mixing[:, :modes], low_co)
    high_mix = dot_nn(mixing[:, modes:], high_co)
    mine_split = split_two(jnp.where(first, low_mix, high_mix))
    other_split = split_two(jnp.where(first, high_mix, low_mix))
    piece_refs, rest_refs = out_refs[:-2], out_refs[-2:]
    chunk = piece_refs[0].shape[1]
    split = jnp.concatenate([mine_split, other_split], axis=1)
    for fetch in fetches:
        fetch.wait()
    for i, piece_ref in enumerate(piece_refs):
        here = pl.ds(pl.multiple_of((place_ref[1] ^ i) * chunk, chunk), chunk)
        rows = jnp.concatenate([mine_ref[:, here], other_ref[:, here]], axis=0)
        piece = joined(bf16_dot(split, rows)).astype(BF16)
        piece_ref[...] = piece
        for rest_ref, slots in zip(rest_refs, REST_SLOTS):
            if i in slots:
                at = slots.index(i) * modes
                rest_ref[at : at + modes] = piece


NEIGHBOURS = (1, 3)
REST_SLOTS = ((0, 2, 3), (0, 1, 2))


def rows_gram_kernel(place_ref, *refs):
    piece_refs, (_, _, gram_ref, low_rest_ref, high_rest_ref, rows_ref) = refs[:-6], refs[-6:]
    modes = piece_refs[0].shape[0]
    low_rest_ref[3 * modes :] = piece_refs[3][...]
    high_rest_ref[3 * modes :] = piece_refs[1][...]
    for i, piece_ref in enumerate(piece_refs):
        start = pl.multiple_of((place_ref[1] ^ i) * modes, modes)
        rows_ref[pl.ds(start, modes), :] = piece_ref[...]
    rows = rows_ref[...]
    gram = bf16_dot_nt(rows, rows)
    m, h = modes, modes // 2
    gram_ref[:m] = gram[:m]
    gram_ref[m : 2 * m] = gram[m : 2 * m]
    gram_ref[m : 2 * m, :m] = gram[3 * m :, 3 * m :]
    gram_ref[2 * m :, : 2 * m] = gram[2 * m : 2 * m + h, 2 * m :]
    gram_ref[2 * m :, 2 * m :] = gram[2 * m + h : 3 * m, 2 * m :]


def tree_kernel(gram_ref, mix_ref, whole_ref):
    mix = mix_ref[...]
    m = mix.shape[1]
    h = m // 2
    top = gram_ref[:m]
    second = gram_ref[m : 2 * m]
    third = gram_ref[2 * m :]
    low = stack_gram(top[:, :m], top[:, m : 2 * m], top[:, m : 2 * m].T, second[:, m : 2 * m])
    third = jnp.concatenate([third[:, : 2 * m], third[:, 2 * m :]], axis=0)
    high = stack_gram(third[:, :m], third[:, m:], third[:, m:].T, second[:, :m])
    cross = jnp.concatenate([top[:, 2 * m :], second[:, 2 * m :]], axis=0)
    low_mix, high_mix = mixings([low, high], mix)
    gram = stack_gram(
        dot_nt(dot_nn(low_mix, low), low_mix),
        dot_nt(dot_nn(low_mix, cross), high_mix),
        dot_nt(dot_nt(high_mix, cross), low_mix),
        dot_nt(dot_nn(high_mix, high), high_mix),
    )
    last = mixings([gram], mix)[0]
    whole_ref[...] = jnp.concatenate(
        [dot_nn(last[:, :m], low_mix), dot_nn(last[:, m:], high_mix)], axis=1
    )


def finish_kernel(place_ref, whole_ref, *refs):
    own_refs, got_refs = refs[:4], refs[4:7]
    far_ref, low_rest_ref, high_rest_ref, keep_ref, give_ref = refs[7:]
    chips = len(own_refs)
    core, chip = place_ref[0], place_ref[1]
    modes, chunk = own_refs[0].shape
    own = 2 * keep_ref.shape[0]
    mixing = whole_ref[pl.ds(pl.multiple_of(chip * own, own), own), :]
    mixing = jnp.where(chip & 2 != 0, pltpu.roll(mixing, 2 * modes, 1), mixing)
    lanes = lax.broadcasted_iota(jnp.int32, mixing.shape, 1)
    turned = jnp.where(
        (lanes // modes) % 2 == 0,
        pltpu.roll(mixing, (chips - 1) * modes, 1),
        pltpu.roll(mixing, modes, 1),
    )
    split = split_two(jnp.where(chip & 1 != 0, turned, mixing))
    for r in range(chips):
        blocks = [own_refs[r][...]]
        if r == 0:
            blocks += [got_ref[...] for got_ref in got_refs]
        else:
            near = [
                rest_ref[slots.index(apart ^ r) * modes : (slots.index(apart ^ r) + 1) * modes]
                for rest_ref, slots, apart in zip((low_rest_ref, high_rest_ref), REST_SLOTS, NEIGHBOURS)
            ]
            far = {1: low_rest_ref[3 * modes :], 2: far_ref[...], 3: high_rest_ref[3 * modes :]}[r]
            blocks += [near[0], far, near[1]]
        part = joined(bf16_dot(split, jnp.concatenate(blocks, axis=0)))
        low, high = part[: own // 2], part[own // 2 :]
        there = pl.ds(pl.multiple_of((chip ^ r) * chunk, chunk), chunk)
        keep_ref[:, there] = jnp.where(core == 0, low, high)
        give_ref[:, there] = jnp.where(core == 0, high, low)


def assemble_kernel(place_ref, keep_ref, got_ref, out_ref):
    core = place_ref[0]
    chips = out_ref.shape[1] // keep_ref.shape[1] * 2
    chunk = keep_ref.shape[1] // chips
    for i in range(chips):
        here = pl.ds(i * chunk, chunk)
        out_ref[:, pl.ds(pl.multiple_of((2 * i + core) * chunk, chunk), chunk)] = keep_ref[:, here]
        out_ref[:, pl.ds(pl.multiple_of((2 * i + 1 - core) * chunk, chunk), chunk)] = got_ref[:, here]


VMEM = pl.BlockSpec(memory_space=pltpu.VMEM)
SMEM = pl.BlockSpec(memory_space=pltpu.SMEM)
HBM_SPACE = pltpu.HBM


def call(kernel, out_shape, in_specs, name, flops=0, scratch=(), vmem=VMEM_LIMIT, aliases=()):
    return pl.pallas_call(
        kernel,
        out_shape=out_shape,
        in_specs=in_specs,
        out_specs=jax.tree.map(lambda _: VMEM, out_shape),
        scratch_shapes=scratch,
        input_output_aliases=dict(aliases),
        compiler_params=pltpu.CompilerParams(vmem_limit_bytes=vmem),
        cost_estimate=pl.CostEstimate(flops=flops, bytes_accessed=0, transcendentals=0),
        name=name,
    )


def swap(block, axis, mask):
    count = lax.axis_size(axis)
    return lax.ppermute(block, axis, [(i, i ^ mask) for i in range(count)])


def butterfly(block, axis, masks):
    for mask in masks:
        block = block + swap(block, axis, mask)
    return block


EARLY = (1, 4)
LATE = (3, 8, 24)


def shards(snaps, sketch, merge_mix):
    width, points = snaps.shape
    modes = sketch.shape[0]
    snap_count = lax.axis_size("snap")
    chunk = points // snap_count
    chips = snap_count // 2
    position = lax.axis_index("snap")
    place = jnp.stack([position % 2, position // 2]).astype(jnp.int32)
    shape = jax.ShapeDtypeStruct

    own_gram, mine, away = call(
        own_gram_kernel,
        (shape((width, 2 * width), F32),) + (shape((width, chips * chunk), snaps.dtype),) * 2,
        [SMEM, pl.BlockSpec(memory_space=HBM_SPACE)],
        "own_gram",
        scratch=[pltpu.SemaphoreType.DMA((2 * chips,))],
        vmem=2 * VMEM_LIMIT,
    )(place, snaps)
    other = swap(away, "snap", 1)
    own_gram = butterfly(own_gram, "space", EARLY)

    cross = call(
        cross_gram_kernel,
        shape((width, 2 * width), F32),
        [SMEM] + [VMEM] * 2,
        "cross_gram",
    )(place, mine, other)
    cross = butterfly(cross, "snap", (1,))
    grams = butterfly(own_gram + cross, "space", LATE)
    crossed = butterfly(grams, "space", EARLY)

    work = 4 * 10**9
    half = call(
        functools.partial(power_kernel, ITERS // 2, False),
        shape((modes, width), F32),
        [VMEM] * 2,
        "power_first",
        work,
    )(grams, sketch)
    coeffs = call(
        functools.partial(power_kernel, ITERS - ITERS // 2, True),
        shape((modes, 2 * width), F32),
        [VMEM] * 2,
        "power_last",
        work,
    )(grams, half)
    other_coeffs = swap(coeffs, "snap", 1)

    piece = shape((modes, chunk), BF16)
    rest = shape((4 * modes, chunk), BF16)
    *pieces, low_rest, high_rest = call(
        merge_kernel,
        (piece,) * chips + (rest,) * 2,
        [SMEM] + [VMEM] * 5 + [pl.BlockSpec(memory_space=HBM_SPACE)],
        "merge",
        scratch=[pltpu.VMEM(other.shape, BF16), pltpu.SemaphoreType.DMA((4,))],
        vmem=2 * VMEM_LIMIT,
    )(place, crossed, coeffs, other_coeffs, merge_mix, mine, other)

    got = [swap(pieces[i], "snap", 2 * i) for i in range(1, chips)]
    gram, low_rest, high_rest = call(
        rows_gram_kernel,
        (shape((5 * modes // 2, chips * modes), F32), rest, rest),
        [SMEM] + [VMEM] * (chips + 2),
        "rows_gram",
        scratch=[pltpu.VMEM((chips * modes, chunk), BF16)],
        aliases={chips + 1: 1, chips + 2: 2},
    )(place, pieces[0], *got, low_rest, high_rest)
    gram = butterfly(gram, "snap", (1,))
    far = swap(pieces[0], "snap", 4)
    low_rest = swap(low_rest, "snap", 2)
    high_rest = swap(high_rest, "snap", 6)
    gram = butterfly(gram, "space", EARLY + LATE)
    gram = butterfly(gram, "snap", (2, 6))

    whole = call(
        tree_kernel, shape((modes, chips * modes), F32), [VMEM] * 2, "tree", 21 * work // 10
    )(gram, merge_mix)
    half_out = shape((modes // snap_count, points // 2), F32)
    keep, give = call(
        finish_kernel,
        (half_out, half_out),
        [SMEM] + [VMEM] * (2 * chips + 3),
        "finish",
    )(place, whole, *pieces, *got, far, low_rest, high_rest)
    return call(
        assemble_kernel,
        shape((modes // snap_count, points), F32),
        [SMEM] + [VMEM] * 2,
        "assemble",
    )(place, keep, swap(give, "snap", 1))


def solution(mesh):
    in_specs = (P("snap", "space"), P(None, "snap"), P())
    out_specs = P("snap", "space")
    return jax.shard_map(shards, mesh=mesh, in_specs=in_specs, out_specs=out_specs, check_vma=False)
```

```python
import functools
import math

import jax
import jax.numpy as jnp
from jax import lax
from jax.experimental import pallas as pl
from jax.experimental.pallas import tpu as pltpu
from jax.sharding import PartitionSpec as P

ITERS = 4
PANEL = 8
F32 = jnp.float32
BF16 = jnp.bfloat16
VMEM_LIMIT = 24 * 1024 * 1024


def dot_nn(a, b):
    return jnp.dot(a, b, precision=lax.Precision.HIGHEST, preferred_element_type=F32)


def dot_nt(a, b):
    return lax.dot_general(
        a, b, (((1,), (1,)), ((), ())), precision=lax.Precision.HIGHEST, preferred_element_type=F32
    )


def dot_tn(a, b):
    return lax.dot_general(
        a, b, (((0,), (0,)), ((), ())), precision=lax.Precision.HIGHEST, preferred_element_type=F32
    )


def eliminate_panel(table, wide, first):
    group, inner = divmod(first, 8)
    shape = table[0].shape
    row_ids = lax.broadcasted_iota(jnp.int32, shape, 0)
    columns = [
        [jnp.broadcast_to(t[:, wide + first + k : wide + first + k + 1], shape) for t in table[group:]]
        for k in range(PANEL)
    ]
    rows = [jnp.broadcast_to(table[group][inner + k : inner + k + 1], shape) for k in range(PANEL)]
    corner = {
        (k, l): jnp.broadcast_to(columns[k][0][inner + l : inner + l + 1], shape)
        for k in range(PANEL)
        for l in range(k, PANEL)
    }
    for k in range(PANEL):
        inverse = 1.0 / corner[k, k]
        factors = [c * inverse for c in columns[k]]
        steps = {l: corner[k, l] * inverse for l in range(k + 1, PANEL)}
        for l in range(k + 1, PANEL):
            for m in range(l, PANEL):
                corner[l, m] = corner[l, m] - steps[l] * corner[k, m]
            columns[l] = [c - f * corner[k, l] for c, f in zip(columns[l], factors)]
            rows[l] = rows[l] - steps[l] * rows[k]
        factors[0] = jnp.where(row_ids > inner + k, factors[0], 0.0)
        for g, f in enumerate(factors):
            table[group + g] = table[group + g] - f * rows[k]


def cholesky_solves(pairs):
    modes = pairs[0][0].shape[0]
    wide = pairs[0][1].shape[1]
    tables = []
    for h, b in pairs:
        table = jnp.concatenate([b, h], axis=1)
        tables.append([table[r : r + 8] for r in range(0, modes, 8)])
    for first in range(0, modes, PANEL):
        for table in tables:
            eliminate_panel(table, wide, first)
    solved = []
    for table in tables:
        whole = jnp.concatenate(table, axis=0)
        below = whole[:, wide:]
        same = lax.broadcasted_iota(jnp.int32, below.shape, 0) == lax.broadcasted_iota(
            jnp.int32, below.shape, 1
        )
        diagonal = jnp.sum(jnp.where(same, below, 0.0), axis=1, keepdims=True)
        solved.append(whole[:, :wide] * lax.rsqrt(diagonal))
    return solved


def trace_scale(gram):
    same = lax.broadcasted_iota(jnp.int32, gram.shape, 0) == lax.broadcasted_iota(
        jnp.int32, gram.shape, 1
    )
    diagonal = jnp.where(same, gram, 0.0)
    return lax.rsqrt(jnp.sum(jnp.sum(diagonal, axis=1, keepdims=True), axis=0, keepdims=True))


def mixings(grams, mix):
    pairs = []
    for gram in grams:
        curved_t = dot_tn(mix, gram)
        pairs.append((dot_nn(curved_t, mix), curved_t))
    return [s * trace_scale(g) for s, g in zip(cholesky_solves(pairs), grams)]


def split_two(x):
    high = x.astype(BF16)
    return jnp.concatenate([high, (x - high.astype(F32)).astype(BF16)], axis=0)


def bf16_dot(a, b):
    return jnp.dot(a, b, preferred_element_type=F32)


def bf16_dot_nt(a, b):
    return lax.dot_general(a, b, (((1,), (1,)), ((), ())), preferred_element_type=F32)


def joined(both):
    modes = both.shape[0] // 2
    return both[:modes] + both[modes:]


def own_gram_kernel(place_ref, snaps_ref, gram_ref, mine_ref, away_ref, sems):
    core = place_ref[0]
    width, points = mine_ref.shape
    chips = sems.shape[0] // 2
    chunk = points // chips
    parts = []
    for packed_ref, parity in ((mine_ref, core), (away_ref, 1 - core)):
        copies = []
        for i in range(chips):
            there = pl.ds(pl.multiple_of((2 * i + parity) * chunk, chunk), chunk)
            here = pl.ds(i * chunk, chunk)
            sem = sems.at[len(parts) * chips + i]
            copies.append(pltpu.make_async_copy(snaps_ref.at[:, there], packed_ref.at[:, here], sem))
        parts.append((packed_ref, copies))
    for _, copies in parts:
        for copy in copies:
            copy.start()
    grams = []
    for packed_ref, copies in parts:
        for copy in copies:
            copy.wait()
        rows = packed_ref[...]
        grams.append(bf16_dot_nt(rows, rows))
    gram_ref[...] = jnp.zeros_like(gram_ref)
    gram_ref[:, :width] = grams[0] + grams[1]


def cross_gram_kernel(place_ref, mine_ref, other_ref, gram_ref):
    width = mine_ref.shape[0]
    gram_ref[...] = jnp.zeros_like(gram_ref)

    @pl.when(place_ref[0] == 0)
    def _():
        gram_ref[:, width:] = bf16_dot_nt(mine_ref[...], other_ref[...])

    @pl.when(place_ref[0] != 0)
    def _():
        gram_ref[:, width:] = bf16_dot_nt(other_ref[...], mine_ref[...])


def power_kernel(iters, last, gram_ref, coeffs_ref, out_ref):
    coeffs = coeffs_ref[...].astype(F32)
    width = coeffs.shape[1]
    modes = coeffs.shape[0]
    gram = gram_ref[:, :width]
    scale = 1.0 / math.sqrt(width)
    for _ in range(iters):
        weighted = dot_nn(coeffs, gram)
        solved = cholesky_solves([(dot_nt(weighted, coeffs), weighted)])[0]
        coeffs = solved.astype(BF16).astype(F32) * scale
    if last:
        out_ref[...] = jnp.zeros_like(out_ref)
        out_ref[:, :width] = coeffs
        out_ref[:, width : width + modes] = dot_nt(dot_nn(coeffs, gram), coeffs)
    else:
        out_ref[...] = coeffs


def stack_gram(low, cross, cross_t, high):
    return jnp.concatenate(
        [jnp.concatenate([low, cross], axis=1), jnp.concatenate([cross_t, high], axis=1)], axis=0
    )


def merge_kernel(place_ref, cross_ref, mine_co_ref, other_co_ref, mix_ref, mine_ref, other_hbm, *refs):
    out_refs, (other_ref, sem) = refs[:-2], refs[-2:]
    parts = sem.shape[0]
    part = other_ref.shape[0] // parts
    fetches = [
        pltpu.make_async_copy(other_hbm.at[pl.ds(i * part, part)], other_ref.at[pl.ds(i * part, part)], sem.at[i])
        for i in range(parts)
    ]
    for fetch in fetches:
        fetch.start()
    first = place_ref[0] == 0
    width = mine_ref.shape[0]
    modes = mine_co_ref.shape[0]
    mine_co, other_co = mine_co_ref[...], other_co_ref[...]
    low = jnp.where(first, mine_co, other_co)
    high = jnp.where(first, other_co, mine_co)
    low_co, high_co = low[:, :width], high[:, :width]
    cross = cross_ref[:, width:]
    gram = stack_gram(
        low[:, width : width + modes],
        dot_nt(dot_nn(low_co, cross), high_co),
        dot_nt(dot_nt(high_co, cross), low_co),
        high[:, width : width + modes],
    )
    mixing = mixings([gram], mix_ref[...])[0]
    low_mix = dot_nn(mixing[:, :modes], low_co)
    high_mix = dot_nn(mixing[:, modes:], high_co)
    mine_split = split_two(jnp.where(first, low_mix, high_mix))
    other_split = split_two(jnp.where(first, high_mix, low_mix))
    piece_refs, rest_refs = out_refs[:-2], out_refs[-2:]
    chunk = piece_refs[0].shape[1]
    split = jnp.concatenate([mine_split, other_split], axis=1)
    for fetch in fetches:
        fetch.wait()
    for i, piece_ref in enumerate(piece_refs):
        here = pl.ds(pl.multiple_of((place_ref[1] ^ i) * chunk, chunk), chunk)
        rows = jnp.concatenate([mine_ref[:, here], other_ref[:, here]], axis=0)
        piece = joined(bf16_dot(split, rows)).astype(BF16)
        piece_ref[...] = piece
        for rest_ref, slots in zip(rest_refs, REST_SLOTS):
            if i in slots:
                at = slots.index(i) * modes
                rest_ref[at : at + modes] = piece


NEIGHBOURS = (1, 3)
REST_SLOTS = ((0, 2, 3), (0, 1, 2))


def rows_gram_kernel(place_ref, *refs):
    piece_refs, (_, _, gram_ref, low_rest_ref, high_rest_ref, rows_ref) = refs[:-6], refs[-6:]
    modes = piece_refs[0].shape[0]
    low_rest_ref[3 * modes :] = piece_refs[3][...]
    high_rest_ref[3 * modes :] = piece_refs[1][...]
    for i, piece_ref in enumerate(piece_refs):
        start = pl.multiple_of((place_ref[1] ^ i) * modes, modes)
        rows_ref[pl.ds(start, modes), :] = piece_ref[...]
    rows = rows_ref[...]
    gram = bf16_dot_nt(rows, rows)
    m, h = modes, modes // 2
    gram_ref[:m] = gram[:m]
    gram_ref[m : 2 * m] = gram[m : 2 * m]
    gram_ref[m : 2 * m, :m] = gram[3 * m :, 3 * m :]
    gram_ref[2 * m :, : 2 * m] = gram[2 * m : 2 * m + h, 2 * m :]
    gram_ref[2 * m :, 2 * m :] = gram[2 * m + h : 3 * m, 2 * m :]


def tree_kernel(gram_ref, mix_ref, whole_ref):
    mix = mix_ref[...]
    m = mix.shape[1]
    h = m // 2
    top = gram_ref[:m]
    second = gram_ref[m : 2 * m]
    third = gram_ref[2 * m :]
    low = stack_gram(top[:, :m], top[:, m : 2 * m], top[:, m : 2 * m].T, second[:, m : 2 * m])
    third = jnp.concatenate([third[:, : 2 * m], third[:, 2 * m :]], axis=0)
    high = stack_gram(third[:, :m], third[:, m:], third[:, m:].T, second[:, :m])
    cross = jnp.concatenate([top[:, 2 * m :], second[:, 2 * m :]], axis=0)
    low_mix, high_mix = mixings([low, high], mix)
    gram = stack_gram(
        dot_nt(dot_nn(low_mix, low), low_mix),
        dot_nt(dot_nn(low_mix, cross), high_mix),
        dot_nt(dot_nt(high_mix, cross), low_mix),
        dot_nt(dot_nn(high_mix, high), high_mix),
    )
    last = mixings([gram], mix)[0]
    whole_ref[...] = jnp.concatenate(
        [dot_nn(last[:, :m], low_mix), dot_nn(last[:, m:], high_mix)], axis=1
    )


def finish_kernel(place_ref, whole_ref, *refs):
    own_refs, got_refs = refs[:4], refs[4:7]
    far_ref, low_rest_ref, high_rest_ref, keep_ref, give_ref = refs[7:]
    chips = len(own_refs)
    core, chip = place_ref[0], place_ref[1]
    modes, chunk = own_refs[0].shape
    own = 2 * keep_ref.shape[0]
    mixing = whole_ref[pl.ds(pl.multiple_of(chip * own, own), own), :]
    mixing = jnp.where(chip & 2 != 0, pltpu.roll(mixing, 2 * modes, 1), mixing)
    lanes = lax.broadcasted_iota(jnp.int32, mixing.shape, 1)
    turned = jnp.where(
        (lanes // modes) % 2 == 0,
        pltpu.roll(mixing, (chips - 1) * modes, 1),
        pltpu.roll(mixing, modes, 1),
    )
    split = split_two(jnp.where(chip & 1 != 0, turned, mixing))
    for r in range(chips):
        blocks = [own_refs[r][...]]
        if r == 0:
            blocks += [got_ref[...] for got_ref in got_refs]
        else:
            near = [
                rest_ref[slots.index(apart ^ r) * modes : (slots.index(apart ^ r) + 1) * modes]
                for rest_ref, slots, apart in zip((low_rest_ref, high_rest_ref), REST_SLOTS, NEIGHBOURS)
            ]
            far = {1: low_rest_ref[3 * modes :], 2: far_ref[...], 3: high_rest_ref[3 * modes :]}[r]
            blocks += [near[0], far, near[1]]
        part = joined(bf16_dot(split, jnp.concatenate(blocks, axis=0)))
        low, high = part[: own // 2], part[own // 2 :]
        there = pl.ds(pl.multiple_of((chip ^ r) * chunk, chunk), chunk)
        keep_ref[:, there] = jnp.where(core == 0, low, high)
        give_ref[:, there] = jnp.where(core == 0, high, low)


def assemble_kernel(place_ref, keep_ref, got_ref, out_ref):
    core = place_ref[0]
    chips = out_ref.shape[1] // keep_ref.shape[1] * 2
    chunk = keep_ref.shape[1] // chips
    for i in range(chips):
        here = pl.ds(i * chunk, chunk)
        out_ref[:, pl.ds(pl.multiple_of((2 * i + core) * chunk, chunk), chunk)] = keep_ref[:, here]
        out_ref[:, pl.ds(pl.multiple_of((2 * i + 1 - core) * chunk, chunk), chunk)] = got_ref[:, here]


VMEM = pl.BlockSpec(memory_space=pltpu.VMEM)
SMEM = pl.BlockSpec(memory_space=pltpu.SMEM)
HBM_SPACE = pltpu.HBM


def call(kernel, out_shape, in_specs, name, flops=0, scratch=(), vmem=VMEM_LIMIT, aliases=()):
    return pl.pallas_call(
        kernel,
        out_shape=out_shape,
        in_specs=in_specs,
        out_specs=jax.tree.map(lambda _: VMEM, out_shape),
        scratch_shapes=scratch,
        input_output_aliases=dict(aliases),
        compiler_params=pltpu.CompilerParams(vmem_limit_bytes=vmem),
        cost_estimate=pl.CostEstimate(flops=flops, bytes_accessed=0, transcendentals=0),
        name=name,
    )


def swap(block, axis, mask):
    count = lax.axis_size(axis)
    return lax.ppermute(block, axis, [(i, i ^ mask) for i in range(count)])


def butterfly(block, axis, masks):
    for mask in masks:
        block = block + swap(block, axis, mask)
    return block


EARLY = (1, 4)
LATE = (3, 8, 24)


def shards(snaps, sketch, merge_mix):
    width, points = snaps.shape
    modes = sketch.shape[0]
    snap_count = lax.axis_size("snap")
    chunk = points // snap_count
    chips = snap_count // 2
    position = lax.axis_index("snap")
    place = jnp.stack([position % 2, position // 2]).astype(jnp.int32)
    shape = jax.ShapeDtypeStruct

    own_gram, mine, away = call(
        own_gram_kernel,
        (shape((width, 2 * width), F32),) + (shape((width, chips * chunk), snaps.dtype),) * 2,
        [SMEM, pl.BlockSpec(memory_space=HBM_SPACE)],
        "own_gram",
        scratch=[pltpu.SemaphoreType.DMA((2 * chips,))],
        vmem=2 * VMEM_LIMIT,
    )(place, snaps)
    other = swap(away, "snap", 1)
    own_gram = butterfly(own_gram, "space", EARLY)

    cross = call(
        cross_gram_kernel,
        shape((width, 2 * width), F32),
        [SMEM] + [VMEM] * 2,
        "cross_gram",
    )(place, mine, other)
    grams = butterfly(own_gram + cross, "space", LATE)
    crossed = butterfly(grams, "space", EARLY)

    work = 4 * 10**9
    half = call(
        functools.partial(power_kernel, ITERS // 2, False),
        shape((modes, width), F32),
        [VMEM] * 2,
        "power_first",
        work,
    )(grams, sketch)
    coeffs = call(
        functools.partial(power_kernel, ITERS - ITERS // 2, True),
        shape((modes, 2 * width), F32),
        [VMEM] * 2,
        "power_last",
        work,
    )(grams, half)
    crossed, coeffs = lax.optimization_barrier((crossed, coeffs))
    other_coeffs = swap(coeffs, "snap", 1)
    crossed = butterfly(crossed, "snap", (1,))

    piece = shape((modes, chunk), BF16)
    rest = shape((4 * modes, chunk), BF16)
    *pieces, low_rest, high_rest = call(
        merge_kernel,
        (piece,) * chips + (rest,) * 2,
        [SMEM] + [VMEM] * 5 + [pl.BlockSpec(memory_space=HBM_SPACE)],
        "merge",
        scratch=[pltpu.VMEM(other.shape, BF16), pltpu.SemaphoreType.DMA((4,))],
        vmem=2 * VMEM_LIMIT,
    )(place, crossed, coeffs, other_coeffs, merge_mix, mine, other)

    got = [swap(pieces[i], "snap", 2 * i) for i in range(1, chips)]
    gram, low_rest, high_rest = call(
        rows_gram_kernel,
        (shape((5 * modes // 2, chips * modes), F32), rest, rest),
        [SMEM] + [VMEM] * (chips + 2),
        "rows_gram",
        scratch=[pltpu.VMEM((chips * modes, chunk), BF16)],
        aliases={chips + 1: 1, chips + 2: 2},
    )(place, pieces[0], *got, low_rest, high_rest)
    gram = butterfly(gram, "snap", (1,))
    low_rest = swap(low_rest, "snap", 2)
    high_rest = swap(high_rest, "snap", 6)
    gram, far = lax.optimization_barrier((gram, pieces[0]))
    far = swap(far, "snap", 4)
    gram = butterfly(gram, "space", EARLY + LATE)
    gram = butterfly(gram, "snap", (2, 6))
    gram, far = lax.optimization_barrier((gram, far))

    whole = call(
        tree_kernel, shape((modes, chips * modes), F32), [VMEM] * 2, "tree", 21 * work // 10
    )(gram, merge_mix)
    half_out = shape((modes // snap_count, points // 2), F32)
    keep, give = call(
        finish_kernel,
        (half_out, half_out),
        [SMEM] + [VMEM] * (2 * chips + 3),
        "finish",
    )(place, whole, *pieces, *got, far, low_rest, high_rest)
    return call(
        assemble_kernel,
        shape((modes // snap_count, points), F32),
        [SMEM] + [VMEM] * 2,
        "assemble",
    )(place, keep, swap(give, "snap", 1))


def solution(mesh):
    in_specs = (P("snap", "space"), P(None, "snap"), P())
    out_specs = P("snap", "space")
    return jax.shard_map(shards, mesh=mesh, in_specs=in_specs, out_specs=out_specs, check_vma=False)
```

```python
import functools
import math

import jax
import jax.numpy as jnp
from jax import lax
from jax.experimental import pallas as pl
from jax.experimental.pallas import tpu as pltpu
from jax.sharding import PartitionSpec as P

ITERS = 4
PANEL = 8
F32 = jnp.float32
BF16 = jnp.bfloat16
VMEM_LIMIT = 24 * 1024 * 1024


def dot_nn(a, b):
    return jnp.dot(a, b, precision=lax.Precision.HIGHEST, preferred_element_type=F32)


def dot_nt(a, b):
    return lax.dot_general(
        a, b, (((1,), (1,)), ((), ())), precision=lax.Precision.HIGHEST, preferred_element_type=F32
    )


def dot_tn(a, b):
    return lax.dot_general(
        a, b, (((0,), (0,)), ((), ())), precision=lax.Precision.HIGHEST, preferred_element_type=F32
    )


def eliminate_panel(table, wide, first):
    group, inner = divmod(first, 8)
    shape = table[0].shape
    row_ids = lax.broadcasted_iota(jnp.int32, shape, 0)
    columns = [
        [jnp.broadcast_to(t[:, wide + first + k : wide + first + k + 1], shape) for t in table[group:]]
        for k in range(PANEL)
    ]
    rows = [jnp.broadcast_to(table[group][inner + k : inner + k + 1], shape) for k in range(PANEL)]
    corner = {
        (k, l): jnp.broadcast_to(columns[k][0][inner + l : inner + l + 1], shape)
        for k in range(PANEL)
        for l in range(k, PANEL)
    }
    for k in range(PANEL):
        inverse = 1.0 / corner[k, k]
        factors = [c * inverse for c in columns[k]]
        steps = {l: corner[k, l] * inverse for l in range(k + 1, PANEL)}
        for l in range(k + 1, PANEL):
            for m in range(l, PANEL):
                corner[l, m] = corner[l, m] - steps[l] * corner[k, m]
            columns[l] = [c - f * corner[k, l] for c, f in zip(columns[l], factors)]
            rows[l] = rows[l] - steps[l] * rows[k]
        factors[0] = jnp.where(row_ids > inner + k, factors[0], 0.0)
        for g, f in enumerate(factors):
            table[group + g] = table[group + g] - f * rows[k]


def cholesky_solves(pairs):
    modes = pairs[0][0].shape[0]
    wide = pairs[0][1].shape[1]
    tables = []
    for h, b in pairs:
        table = jnp.concatenate([b, h], axis=1)
        tables.append([table[r : r + 8] for r in range(0, modes, 8)])
    for first in range(0, modes, PANEL):
        for table in tables:
            eliminate_panel(table, wide, first)
    solved = []
    for table in tables:
        whole = jnp.concatenate(table, axis=0)
        below = whole[:, wide:]
        same = lax.broadcasted_iota(jnp.int32, below.shape, 0) == lax.broadcasted_iota(
            jnp.int32, below.shape, 1
        )
        diagonal = jnp.sum(jnp.where(same, below, 0.0), axis=1, keepdims=True)
        solved.append(whole[:, :wide] * lax.rsqrt(diagonal))
    return solved


def trace_scale(gram):
    same = lax.broadcasted_iota(jnp.int32, gram.shape, 0) == lax.broadcasted_iota(
        jnp.int32, gram.shape, 1
    )
    diagonal = jnp.where(same, gram, 0.0)
    return lax.rsqrt(jnp.sum(jnp.sum(diagonal, axis=1, keepdims=True), axis=0, keepdims=True))


def mixings(grams, mix):
    pairs = []
    for gram in grams:
        curved_t = dot_tn(mix, gram)
        pairs.append((dot_nn(curved_t, mix), curved_t))
    return [s * trace_scale(g) for s, g in zip(cholesky_solves(pairs), grams)]


def split_two(x):
    high = x.astype(BF16)
    return jnp.concatenate([high, (x - high.astype(F32)).astype(BF16)], axis=0)


def bf16_dot(a, b):
    return jnp.dot(a, b, preferred_element_type=F32)


def bf16_dot_nt(a, b):
    return lax.dot_general(a, b, (((1,), (1,)), ((), ())), preferred_element_type=F32)


def joined(both):
    modes = both.shape[0] // 2
    return both[:modes] + both[modes:]


def own_gram_kernel(place_ref, snaps_ref, gram_ref, mine_ref, away_ref, sems):
    core = place_ref[0]
    width, points = mine_ref.shape
    chips = sems.shape[0] // 2
    chunk = points // chips
    parts = []
    for packed_ref, parity in ((mine_ref, core), (away_ref, 1 - core)):
        copies = []
        for i in range(chips):
            there = pl.ds(pl.multiple_of((2 * i + parity) * chunk, chunk), chunk)
            here = pl.ds(i * chunk, chunk)
            sem = sems.at[len(parts) * chips + i]
            copies.append(pltpu.make_async_copy(snaps_ref.at[:, there], packed_ref.at[:, here], sem))
        parts.append((packed_ref, copies))
    for _, copies in parts:
        for copy in copies:
            copy.start()
    grams = []
    for packed_ref, copies in parts:
        for copy in copies:
            copy.wait()
        rows = packed_ref[...]
        grams.append(bf16_dot_nt(rows, rows))
    gram_ref[...] = jnp.zeros_like(gram_ref)
    gram_ref[:, :width] = grams[0] + grams[1]


def cross_gram_kernel(place_ref, mine_ref, other_ref, gram_ref):
    width = mine_ref.shape[0]
    gram_ref[...] = jnp.zeros_like(gram_ref)

    @pl.when(place_ref[0] == 0)
    def _():
        gram_ref[:, width:] = bf16_dot_nt(mine_ref[...], other_ref[...])

    @pl.when(place_ref[0] != 0)
    def _():
        gram_ref[:, width:] = bf16_dot_nt(other_ref[...], mine_ref[...])


def power_kernel(iters, last, gram_ref, coeffs_ref, out_ref):
    coeffs = coeffs_ref[...].astype(F32)
    width = coeffs.shape[1]
    modes = coeffs.shape[0]
    gram = gram_ref[:, :width]
    scale = 1.0 / math.sqrt(width)
    for _ in range(iters):
        weighted = dot_nn(coeffs, gram)
        solved = cholesky_solves([(dot_nt(weighted, coeffs), weighted)])[0]
        coeffs = solved.astype(BF16).astype(F32) * scale
    if last:
        out_ref[...] = jnp.zeros_like(out_ref)
        out_ref[:, :width] = coeffs
        out_ref[:, width : width + modes] = dot_nt(dot_nn(coeffs, gram), coeffs)
    else:
        out_ref[...] = coeffs


def stack_gram(low, cross, cross_t, high):
    return jnp.concatenate(
        [jnp.concatenate([low, cross], axis=1), jnp.concatenate([cross_t, high], axis=1)], axis=0
    )


def merge_kernel(place_ref, cross_ref, mine_co_ref, other_co_ref, mix_ref, mine_ref, other_hbm, *refs):
    out_refs, (other_ref, sem) = refs[:-2], refs[-2:]
    parts = sem.shape[0]
    part = other_ref.shape[0] // parts
    fetches = [
        pltpu.make_async_copy(other_hbm.at[pl.ds(i * part, part)], other_ref.at[pl.ds(i * part, part)], sem.at[i])
        for i in range(parts)
    ]
    for fetch in fetches:
        fetch.start()
    first = place_ref[0] == 0
    width = mine_ref.shape[0]
    modes = mine_co_ref.shape[0]
    mine_co, other_co = mine_co_ref[...], other_co_ref[...]
    low = jnp.where(first, mine_co, other_co)
    high = jnp.where(first, other_co, mine_co)
    low_co, high_co = low[:, :width], high[:, :width]
    cross = cross_ref[:, width:]
    gram = stack_gram(
        low[:, width : width + modes],
        dot_nt(dot_nn(low_co, cross), high_co),
        dot_nt(dot_nt(high_co, cross), low_co),
        high[:, width : width + modes],
    )
    mixing = mixings([gram], mix_ref[...])[0]
    low_mix = dot_nn(mixing[:, :modes], low_co)
    high_mix = dot_nn(mixing[:, modes:], high_co)
    mine_split = split_two(jnp.where(first, low_mix, high_mix))
    other_split = split_two(jnp.where(first, high_mix, low_mix))
    piece_refs, rest_refs = out_refs[:-2], out_refs[-2:]
    chunk = piece_refs[0].shape[1]
    split = jnp.concatenate([mine_split, other_split], axis=1)
    for fetch in fetches:
        fetch.wait()
    for i, piece_ref in enumerate(piece_refs):
        here = pl.ds(pl.multiple_of((place_ref[1] ^ i) * chunk, chunk), chunk)
        rows = jnp.concatenate([mine_ref[:, here], other_ref[:, here]], axis=0)
        piece = joined(bf16_dot(split, rows)).astype(BF16)
        piece_ref[...] = piece
        for rest_ref, slots in zip(rest_refs, REST_SLOTS):
            if i in slots:
                at = slots.index(i) * modes
                rest_ref[at : at + modes] = piece


NEIGHBOURS = (1, 3)
REST_SLOTS = ((0, 2, 3), (0, 1, 2))


def rows_gram_kernel(place_ref, *refs):
    piece_refs, (_, _, gram_ref, low_rest_ref, high_rest_ref, rows_ref) = refs[:-6], refs[-6:]
    modes = piece_refs[0].shape[0]
    low_rest_ref[3 * modes :] = piece_refs[3][...]
    high_rest_ref[3 * modes :] = piece_refs[1][...]
    for i, piece_ref in enumerate(piece_refs):
        start = pl.multiple_of((place_ref[1] ^ i) * modes, modes)
        rows_ref[pl.ds(start, modes), :] = piece_ref[...]
    rows = rows_ref[...]
    gram = bf16_dot_nt(rows, rows)
    m, h = modes, modes // 2
    gram_ref[:m] = gram[:m]
    gram_ref[m : 2 * m] = gram[m : 2 * m]
    gram_ref[m : 2 * m, :m] = gram[3 * m :, 3 * m :]
    gram_ref[2 * m :, : 2 * m] = gram[2 * m : 2 * m + h, 2 * m :]
    gram_ref[2 * m :, 2 * m :] = gram[2 * m + h : 3 * m, 2 * m :]


def tree_kernel(gram_ref, mix_ref, whole_ref):
    mix = mix_ref[...]
    m = mix.shape[1]
    h = m // 2
    top = gram_ref[:m]
    second = gram_ref[m : 2 * m]
    third = gram_ref[2 * m :]
    low = stack_gram(top[:, :m], top[:, m : 2 * m], top[:, m : 2 * m].T, second[:, m : 2 * m])
    third = jnp.concatenate([third[:, : 2 * m], third[:, 2 * m :]], axis=0)
    high = stack_gram(third[:, :m], third[:, m:], third[:, m:].T, second[:, :m])
    cross = jnp.concatenate([top[:, 2 * m :], second[:, 2 * m :]], axis=0)
    low_mix, high_mix = mixings([low, high], mix)
    gram = stack_gram(
        dot_nt(dot_nn(low_mix, low), low_mix),
        dot_nt(dot_nn(low_mix, cross), high_mix),
        dot_nt(dot_nt(high_mix, cross), low_mix),
        dot_nt(dot_nn(high_mix, high), high_mix),
    )
    last = mixings([gram], mix)[0]
    whole_ref[...] = jnp.concatenate(
        [dot_nn(last[:, :m], low_mix), dot_nn(last[:, m:], high_mix)], axis=1
    )


def finish_kernel(place_ref, whole_ref, *refs):
    own_refs, got_refs = refs[:4], refs[4:7]
    far_ref, low_rest_ref, high_rest_ref, keep_ref, give_ref = refs[7:]
    chips = len(own_refs)
    core, chip = place_ref[0], place_ref[1]
    modes, chunk = own_refs[0].shape
    own = 2 * keep_ref.shape[0]
    mixing = whole_ref[pl.ds(pl.multiple_of(chip * own, own), own), :]
    mixing = jnp.where(chip & 2 != 0, pltpu.roll(mixing, 2 * modes, 1), mixing)
    lanes = lax.broadcasted_iota(jnp.int32, mixing.shape, 1)
    turned = jnp.where(
        (lanes // modes) % 2 == 0,
        pltpu.roll(mixing, (chips - 1) * modes, 1),
        pltpu.roll(mixing, modes, 1),
    )
    split = split_two(jnp.where(chip & 1 != 0, turned, mixing))
    for r in range(chips):
        blocks = [own_refs[r][...]]
        if r == 0:
            blocks += [got_ref[...] for got_ref in got_refs]
        else:
            near = [
                rest_ref[slots.index(apart ^ r) * modes : (slots.index(apart ^ r) + 1) * modes]
                for rest_ref, slots, apart in zip((low_rest_ref, high_rest_ref), REST_SLOTS, NEIGHBOURS)
            ]
            far = {1: low_rest_ref[3 * modes :], 2: far_ref[...], 3: high_rest_ref[3 * modes :]}[r]
            blocks += [near[0], far, near[1]]
        part = joined(bf16_dot(split, jnp.concatenate(blocks, axis=0)))
        low, high = part[: own // 2], part[own // 2 :]
        there = pl.ds(pl.multiple_of((chip ^ r) * chunk, chunk), chunk)
        keep_ref[:, there] = jnp.where(core == 0, low, high)
        give_ref[:, there] = jnp.where(core == 0, high, low)


def assemble_kernel(place_ref, keep_ref, got_ref, out_ref):
    core = place_ref[0]
    chips = out_ref.shape[1] // keep_ref.shape[1] * 2
    chunk = keep_ref.shape[1] // chips
    for i in range(chips):
        here = pl.ds(i * chunk, chunk)
        out_ref[:, pl.ds(pl.multiple_of((2 * i + core) * chunk, chunk), chunk)] = keep_ref[:, here]
        out_ref[:, pl.ds(pl.multiple_of((2 * i + 1 - core) * chunk, chunk), chunk)] = got_ref[:, here]


VMEM = pl.BlockSpec(memory_space=pltpu.VMEM)
SMEM = pl.BlockSpec(memory_space=pltpu.SMEM)
HBM_SPACE = pltpu.HBM


def call(kernel, out_shape, in_specs, name, flops=0, scratch=(), vmem=VMEM_LIMIT, aliases=()):
    return pl.pallas_call(
        kernel,
        out_shape=out_shape,
        in_specs=in_specs,
        out_specs=jax.tree.map(lambda _: VMEM, out_shape),
        scratch_shapes=scratch,
        input_output_aliases=dict(aliases),
        compiler_params=pltpu.CompilerParams(vmem_limit_bytes=vmem),
        cost_estimate=pl.CostEstimate(flops=flops, bytes_accessed=0, transcendentals=0),
        name=name,
    )


def swap(block, axis, mask):
    count = lax.axis_size(axis)
    return lax.ppermute(block, axis, [(i, i ^ mask) for i in range(count)])


def butterfly(block, axis, masks):
    for mask in masks:
        block = block + swap(block, axis, mask)
    return block


EARLY = (1, 4)
LATE = (3, 8, 24)


def shards(snaps, sketch, merge_mix):
    width, points = snaps.shape
    modes = sketch.shape[0]
    snap_count = lax.axis_size("snap")
    chunk = points // snap_count
    chips = snap_count // 2
    position = lax.axis_index("snap")
    place = jnp.stack([position % 2, position // 2]).astype(jnp.int32)
    shape = jax.ShapeDtypeStruct

    own_gram, mine, away = call(
        own_gram_kernel,
        (shape((width, 2 * width), F32),) + (shape((width, chips * chunk), snaps.dtype),) * 2,
        [SMEM, pl.BlockSpec(memory_space=HBM_SPACE)],
        "own_gram",
        scratch=[pltpu.SemaphoreType.DMA((2 * chips,))],
        vmem=2 * VMEM_LIMIT,
    )(place, snaps)
    other = swap(away, "snap", 1)
    own_gram = butterfly(own_gram, "space", EARLY)

    cross = call(
        cross_gram_kernel,
        shape((width, 2 * width), F32),
        [SMEM] + [VMEM] * 2,
        "cross_gram",
    )(place, mine, other)
    cross = butterfly(cross, "snap", (1,))
    grams = butterfly(own_gram + cross, "space", LATE)
    crossed = butterfly(grams, "space", EARLY)

    work = 4 * 10**9
    half = call(
        functools.partial(power_kernel, ITERS // 2, False),
        shape((modes, width), F32),
        [VMEM] * 2,
        "power_first",
        work,
    )(grams, sketch)
    coeffs = call(
        functools.partial(power_kernel, ITERS - ITERS // 2, True),
        shape((modes, 2 * width), F32),
        [VMEM] * 2,
        "power_last",
        work,
    )(grams, half)
    other_coeffs = swap(coeffs, "snap", 1)

    piece = shape((modes, chunk), BF16)
    rest = shape((4 * modes, chunk), BF16)
    *pieces, low_rest, high_rest = call(
        merge_kernel,
        (piece,) * chips + (rest,) * 2,
        [SMEM] + [VMEM] * 5 + [pl.BlockSpec(memory_space=HBM_SPACE)],
        "merge",
        scratch=[pltpu.VMEM(other.shape, BF16), pltpu.SemaphoreType.DMA((4,))],
        vmem=2 * VMEM_LIMIT,
    )(place, crossed, coeffs, other_coeffs, merge_mix, mine, other)

    got = [swap(pieces[i], "snap", 2 * i) for i in range(1, chips)]
    gram, low_rest, high_rest = call(
        rows_gram_kernel,
        (shape((5 * modes // 2, chips * modes), F32), rest, rest),
        [SMEM] + [VMEM] * (chips + 2),
        "rows_gram",
        scratch=[pltpu.VMEM((chips * modes, chunk), BF16)],
        aliases={chips + 1: 1, chips + 2: 2},
    )(place, pieces[0], *got, low_rest, high_rest)
    gram = butterfly(gram, "snap", (1, 2))
    gram, far, low_rest, high_rest = lax.optimization_barrier((gram, pieces[0], low_rest, high_rest))
    far = swap(far, "snap", 4)
    low_rest = swap(low_rest, "snap", 2)
    high_rest = swap(high_rest, "snap", 6)
    gram = butterfly(gram, "snap", (6,))
    gram = butterfly(gram, "space", EARLY + LATE)

    whole = call(
        tree_kernel, shape((modes, chips * modes), F32), [VMEM] * 2, "tree", 22 * work // 10
    )(gram, merge_mix)
    half_out = shape((modes // snap_count, points // 2), F32)
    keep, give = call(
        finish_kernel,
        (half_out, half_out),
        [SMEM] + [VMEM] * (2 * chips + 3),
        "finish",
    )(place, whole, *pieces, *got, far, low_rest, high_rest)
    return call(
        assemble_kernel,
        shape((modes // snap_count, points), F32),
        [SMEM] + [VMEM] * 2,
        "assemble",
    )(place, keep, swap(give, "snap", 1))


def solution(mesh):
    in_specs = (P("snap", "space"), P(None, "snap"), P())
    out_specs = P("snap", "space")
    return jax.shard_map(shards, mesh=mesh, in_specs=in_specs, out_specs=out_specs, check_vma=False)
```

```python
import functools
import math

import jax
import jax.numpy as jnp
from jax import lax
from jax.experimental import pallas as pl
from jax.experimental.pallas import tpu as pltpu
from jax.sharding import PartitionSpec as P

ITERS = 4
PANEL = 8
F32 = jnp.float32
BF16 = jnp.bfloat16
VMEM_LIMIT = 24 * 1024 * 1024


def dot_nn(a, b):
    return jnp.dot(a, b, precision=lax.Precision.HIGHEST, preferred_element_type=F32)


def dot_nt(a, b):
    return lax.dot_general(
        a, b, (((1,), (1,)), ((), ())), precision=lax.Precision.HIGHEST, preferred_element_type=F32
    )


def dot_tn(a, b):
    return lax.dot_general(
        a, b, (((0,), (0,)), ((), ())), precision=lax.Precision.HIGHEST, preferred_element_type=F32
    )


def eliminate_panel(table, wide, first):
    group, inner = divmod(first, 8)
    shape = table[0].shape
    row_ids = lax.broadcasted_iota(jnp.int32, shape, 0)
    columns = [
        [jnp.broadcast_to(t[:, wide + first + k : wide + first + k + 1], shape) for t in table[group:]]
        for k in range(PANEL)
    ]
    rows = [jnp.broadcast_to(table[group][inner + k : inner + k + 1], shape) for k in range(PANEL)]
    corner = {
        (k, l): jnp.broadcast_to(columns[k][0][inner + l : inner + l + 1], shape)
        for k in range(PANEL)
        for l in range(k, PANEL)
    }
    for k in range(PANEL):
        inverse = 1.0 / corner[k, k]
        factors = [c * inverse for c in columns[k]]
        steps = {l: corner[k, l] * inverse for l in range(k + 1, PANEL)}
        for l in range(k + 1, PANEL):
            for m in range(l, PANEL):
                corner[l, m] = corner[l, m] - steps[l] * corner[k, m]
            columns[l] = [c - f * corner[k, l] for c, f in zip(columns[l], factors)]
            rows[l] = rows[l] - steps[l] * rows[k]
        factors[0] = jnp.where(row_ids > inner + k, factors[0], 0.0)
        for g, f in enumerate(factors):
            table[group + g] = table[group + g] - f * rows[k]


def cholesky_solves(pairs):
    modes = pairs[0][0].shape[0]
    wide = pairs[0][1].shape[1]
    tables = []
    for h, b in pairs:
        table = jnp.concatenate([b, h], axis=1)
        tables.append([table[r : r + 8] for r in range(0, modes, 8)])
    for first in range(0, modes, PANEL):
        for table in tables:
            eliminate_panel(table, wide, first)
    solved = []
    for table in tables:
        whole = jnp.concatenate(table, axis=0)
        below = whole[:, wide:]
        same = lax.broadcasted_iota(jnp.int32, below.shape, 0) == lax.broadcasted_iota(
            jnp.int32, below.shape, 1
        )
        diagonal = jnp.sum(jnp.where(same, below, 0.0), axis=1, keepdims=True)
        solved.append(whole[:, :wide] * lax.rsqrt(diagonal))
    return solved


def trace_scale(gram):
    same = lax.broadcasted_iota(jnp.int32, gram.shape, 0) == lax.broadcasted_iota(
        jnp.int32, gram.shape, 1
    )
    diagonal = jnp.where(same, gram, 0.0)
    return lax.rsqrt(jnp.sum(jnp.sum(diagonal, axis=1, keepdims=True), axis=0, keepdims=True))


def mixings(grams, mix):
    pairs = []
    for gram in grams:
        curved_t = dot_tn(mix, gram)
        pairs.append((dot_nn(curved_t, mix), curved_t))
    return [s * trace_scale(g) for s, g in zip(cholesky_solves(pairs), grams)]


def split_two(x):
    high = x.astype(BF16)
    return jnp.concatenate([high, (x - high.astype(F32)).astype(BF16)], axis=0)


def bf16_dot(a, b):
    return jnp.dot(a, b, preferred_element_type=F32)


def bf16_dot_nt(a, b):
    return lax.dot_general(a, b, (((1,), (1,)), ((), ())), preferred_element_type=F32)


def joined(both):
    modes = both.shape[0] // 2
    return both[:modes] + both[modes:]


def own_gram_kernel(place_ref, snaps_ref, gram_ref, mine_ref, away_ref, sems):
    core = place_ref[0]
    width, points = mine_ref.shape
    chips = sems.shape[0] // 2
    chunk = points // chips
    parts = []
    for packed_ref, parity in ((mine_ref, core), (away_ref, 1 - core)):
        copies = []
        for i in range(chips):
            there = pl.ds(pl.multiple_of((2 * i + parity) * chunk, chunk), chunk)
            here = pl.ds(i * chunk, chunk)
            sem = sems.at[len(parts) * chips + i]
            copies.append(pltpu.make_async_copy(snaps_ref.at[:, there], packed_ref.at[:, here], sem))
        parts.append((packed_ref, copies))
    for _, copies in parts:
        for copy in copies:
            copy.start()
    grams = []
    for packed_ref, copies in parts:
        for copy in copies:
            copy.wait()
        rows = packed_ref[...]
        grams.append(bf16_dot_nt(rows, rows))
    gram_ref[...] = jnp.zeros_like(gram_ref)
    gram_ref[:, :width] = grams[0] + grams[1]


def cross_gram_kernel(place_ref, mine_ref, other_ref, gram_ref):
    width = mine_ref.shape[0]
    gram_ref[...] = jnp.zeros_like(gram_ref)

    @pl.when(place_ref[0] == 0)
    def _():
        gram_ref[:, width:] = bf16_dot_nt(mine_ref[...], other_ref[...])

    @pl.when(place_ref[0] != 0)
    def _():
        gram_ref[:, width:] = bf16_dot_nt(other_ref[...], mine_ref[...])


def power_kernel(iters, last, gram_ref, coeffs_ref, out_ref):
    coeffs = coeffs_ref[...].astype(F32)
    width = coeffs.shape[1]
    modes = coeffs.shape[0]
    gram = gram_ref[:, :width]
    scale = 1.0 / math.sqrt(width)
    for _ in range(iters):
        weighted = dot_nn(coeffs, gram)
        solved = cholesky_solves([(dot_nt(weighted, coeffs), weighted)])[0]
        coeffs = solved.astype(BF16).astype(F32) * scale
    if last:
        out_ref[...] = jnp.zeros_like(out_ref)
        out_ref[:, :width] = coeffs
        out_ref[:, width : width + modes] = dot_nt(dot_nn(coeffs, gram), coeffs)
    else:
        out_ref[...] = coeffs


def stack_gram(low, cross, cross_t, high):
    return jnp.concatenate(
        [jnp.concatenate([low, cross], axis=1), jnp.concatenate([cross_t, high], axis=1)], axis=0
    )


def merge_kernel(place_ref, cross_ref, mine_co_ref, other_co_ref, mix_ref, mine_ref, other_hbm, *refs):
    out_refs, (other_ref, sem) = refs[:-2], refs[-2:]
    parts = sem.shape[0]
    part = other_ref.shape[0] // parts
    fetches = [
        pltpu.make_async_copy(other_hbm.at[pl.ds(i * part, part)], other_ref.at[pl.ds(i * part, part)], sem.at[i])
        for i in range(parts)
    ]
    for fetch in fetches:
        fetch.start()
    first = place_ref[0] == 0
    width = mine_ref.shape[0]
    modes = mine_co_ref.shape[0]
    mine_co, other_co = mine_co_ref[...], other_co_ref[...]
    low = jnp.where(first, mine_co, other_co)
    high = jnp.where(first, other_co, mine_co)
    low_co, high_co = low[:, :width], high[:, :width]
    cross = cross_ref[:, width:]
    gram = stack_gram(
        low[:, width : width + modes],
        dot_nt(dot_nn(low_co, cross), high_co),
        dot_nt(dot_nt(high_co, cross), low_co),
        high[:, width : width + modes],
    )
    mixing = mixings([gram], mix_ref[...])[0]
    low_mix = dot_nn(mixing[:, :modes], low_co)
    high_mix = dot_nn(mixing[:, modes:], high_co)
    mine_split = split_two(jnp.where(first, low_mix, high_mix))
    other_split = split_two(jnp.where(first, high_mix, low_mix))
    piece_refs, rest_refs = out_refs[:-2], out_refs[-2:]
    chunk = piece_refs[0].shape[1]
    split = jnp.concatenate([mine_split, other_split], axis=1)
    for fetch in fetches:
        fetch.wait()
    for i, piece_ref in enumerate(piece_refs):
        here = pl.ds(pl.multiple_of((place_ref[1] ^ i) * chunk, chunk), chunk)
        rows = jnp.concatenate([mine_ref[:, here], other_ref[:, here]], axis=0)
        piece = joined(bf16_dot(split, rows)).astype(BF16)
        piece_ref[...] = piece
        for rest_ref, slots in zip(rest_refs, REST_SLOTS):
            if i in slots:
                at = slots.index(i) * modes
                rest_ref[at : at + modes] = piece


NEIGHBOURS = (1, 3)
REST_SLOTS = ((0, 2, 3), (0, 1, 2))


def rows_gram_kernel(place_ref, *refs):
    piece_refs, (_, _, gram_ref, low_rest_ref, high_rest_ref, rows_ref) = refs[:-6], refs[-6:]
    modes = piece_refs[0].shape[0]
    low_rest_ref[3 * modes :] = piece_refs[3][...]
    high_rest_ref[3 * modes :] = piece_refs[1][...]
    for i, piece_ref in enumerate(piece_refs):
        start = pl.multiple_of((place_ref[1] ^ i) * modes, modes)
        rows_ref[pl.ds(start, modes), :] = piece_ref[...]
    rows = rows_ref[...]
    gram = bf16_dot_nt(rows, rows)
    m, h = modes, modes // 2
    gram_ref[:m] = gram[:m]
    gram_ref[m : 2 * m] = gram[m : 2 * m]
    gram_ref[m : 2 * m, :m] = gram[3 * m :, 3 * m :]
    gram_ref[2 * m :, : 2 * m] = gram[2 * m : 2 * m + h, 2 * m :]
    gram_ref[2 * m :, 2 * m :] = gram[2 * m + h : 3 * m, 2 * m :]


def tree_kernel(place_ref, mine_ref, other_ref, mix_ref, whole_ref):
    summed = jnp.where(place_ref[0] == 1, mine_ref[...], other_ref[...])
    mix = mix_ref[...]
    m = mix.shape[1]
    h = m // 2
    top, second, third = summed[:m], summed[m : 2 * m], summed[2 * m :]
    low = stack_gram(top[:, :m], top[:, m : 2 * m], top[:, m : 2 * m].T, second[:, m : 2 * m])
    third = jnp.concatenate([third[:, : 2 * m], third[:, 2 * m :]], axis=0)
    high = stack_gram(third[:, :m], third[:, m:], third[:, m:].T, second[:, :m])
    cross = jnp.concatenate([top[:, 2 * m :], second[:, 2 * m :]], axis=0)
    low_mix, high_mix = mixings([low, high], mix)
    gram = stack_gram(
        dot_nt(dot_nn(low_mix, low), low_mix),
        dot_nt(dot_nn(low_mix, cross), high_mix),
        dot_nt(dot_nt(high_mix, cross), low_mix),
        dot_nt(dot_nn(high_mix, high), high_mix),
    )
    last = mixings([gram], mix)[0]
    whole_ref[...] = jnp.concatenate(
        [dot_nn(last[:, :m], low_mix), dot_nn(last[:, m:], high_mix)], axis=1
    )


def finish_kernel(place_ref, whole_ref, *refs):
    own_refs, got_refs = refs[:4], refs[4:7]
    far_ref, low_rest_ref, high_rest_ref, keep_ref, give_ref = refs[7:]
    chips = len(own_refs)
    core, chip = place_ref[0], place_ref[1]
    modes, chunk = own_refs[0].shape
    own = 2 * keep_ref.shape[0]
    mixing = whole_ref[pl.ds(pl.multiple_of(chip * own, own), own), :]
    mixing = jnp.where(chip & 2 != 0, pltpu.roll(mixing, 2 * modes, 1), mixing)
    lanes = lax.broadcasted_iota(jnp.int32, mixing.shape, 1)
    turned = jnp.where(
        (lanes // modes) % 2 == 0,
        pltpu.roll(mixing, (chips - 1) * modes, 1),
        pltpu.roll(mixing, modes, 1),
    )
    split = split_two(jnp.where(chip & 1 != 0, turned, mixing))
    for r in range(chips):
        blocks = [own_refs[r][...]]
        if r == 0:
            blocks += [got_ref[...] for got_ref in got_refs]
        else:
            near = [
                rest_ref[slots.index(apart ^ r) * modes : (slots.index(apart ^ r) + 1) * modes]
                for rest_ref, slots, apart in zip((low_rest_ref, high_rest_ref), REST_SLOTS, NEIGHBOURS)
            ]
            far = {1: low_rest_ref[3 * modes :], 2: far_ref[...], 3: high_rest_ref[3 * modes :]}[r]
            blocks += [near[0], far, near[1]]
        part = joined(bf16_dot(split, jnp.concatenate(blocks, axis=0)))
        low, high = part[: own // 2], part[own // 2 :]
        there = pl.ds(pl.multiple_of((chip ^ r) * chunk, chunk), chunk)
        keep_ref[:, there] = jnp.where(core == 0, low, high)
        give_ref[:, there] = jnp.where(core == 0, high, low)


def assemble_kernel(place_ref, keep_ref, got_ref, out_ref):
    core = place_ref[0]
    chips = out_ref.shape[1] // keep_ref.shape[1] * 2
    chunk = keep_ref.shape[1] // chips
    for i in range(chips):
        here = pl.ds(i * chunk, chunk)
        out_ref[:, pl.ds(pl.multiple_of((2 * i + core) * chunk, chunk), chunk)] = keep_ref[:, here]
        out_ref[:, pl.ds(pl.multiple_of((2 * i + 1 - core) * chunk, chunk), chunk)] = got_ref[:, here]


VMEM = pl.BlockSpec(memory_space=pltpu.VMEM)
SMEM = pl.BlockSpec(memory_space=pltpu.SMEM)
HBM_SPACE = pltpu.HBM


def call(kernel, out_shape, in_specs, name, flops=0, scratch=(), vmem=VMEM_LIMIT, aliases=()):
    return pl.pallas_call(
        kernel,
        out_shape=out_shape,
        in_specs=in_specs,
        out_specs=jax.tree.map(lambda _: VMEM, out_shape),
        scratch_shapes=scratch,
        input_output_aliases=dict(aliases),
        compiler_params=pltpu.CompilerParams(vmem_limit_bytes=vmem),
        cost_estimate=pl.CostEstimate(flops=flops, bytes_accessed=0, transcendentals=0),
        name=name,
    )


def swap(block, axis, mask):
    count = lax.axis_size(axis)
    return lax.ppermute(block, axis, [(i, i ^ mask) for i in range(count)])


def odd_butterfly(block, axis, masks):
    snap_count = lax.axis_size("snap")
    for mask in masks:
        if axis == "snap":
            route = [(i, i ^ mask) for i in range(1, snap_count, 2)]
            got = lax.ppermute(block, "snap", route)
        else:
            places = [(s, i) for s in range(lax.axis_size("space")) for i in range(1, snap_count, 2)]
            route = [(s * snap_count + i, (s ^ mask) * snap_count + i) for s, i in places]
            got = lax.ppermute(block, ("space", "snap"), route)
        block = block + got
    return block


def butterfly(block, axis, masks):
    for mask in masks:
        block = block + swap(block, axis, mask)
    return block


EARLY = (1, 4)
LATE = (3, 8, 24)


def shards(snaps, sketch, merge_mix):
    width, points = snaps.shape
    modes = sketch.shape[0]
    snap_count = lax.axis_size("snap")
    chunk = points // snap_count
    chips = snap_count // 2
    position = lax.axis_index("snap")
    place = jnp.stack([position % 2, position // 2]).astype(jnp.int32)
    shape = jax.ShapeDtypeStruct

    own_gram, mine, away = call(
        own_gram_kernel,
        (shape((width, 2 * width), F32),) + (shape((width, chips * chunk), snaps.dtype),) * 2,
        [SMEM, pl.BlockSpec(memory_space=HBM_SPACE)],
        "own_gram",
        scratch=[pltpu.SemaphoreType.DMA((2 * chips,))],
        vmem=2 * VMEM_LIMIT,
    )(place, snaps)
    other = swap(away, "snap", 1)
    own_gram = butterfly(own_gram, "space", EARLY)

    cross = call(
        cross_gram_kernel,
        shape((width, 2 * width), F32),
        [SMEM] + [VMEM] * 2,
        "cross_gram",
    )(place, mine, other)
    cross = butterfly(cross, "snap", (1,))
    grams = butterfly(own_gram + cross, "space", LATE)
    crossed = butterfly(grams, "space", EARLY)

    work = 4 * 10**9
    half = call(
        functools.partial(power_kernel, ITERS // 2, False),
        shape((modes, width), F32),
        [VMEM] * 2,
        "power_first",
        work,
    )(grams, sketch)
    coeffs = call(
        functools.partial(power_kernel, ITERS - ITERS // 2, True),
        shape((modes, 2 * width), F32),
        [VMEM] * 2,
        "power_last",
        work,
    )(grams, half)
    other_coeffs = swap(coeffs, "snap", 1)

    piece = shape((modes, chunk), BF16)
    rest = shape((4 * modes, chunk), BF16)
    *pieces, low_rest, high_rest = call(
        merge_kernel,
        (piece,) * chips + (rest,) * 2,
        [SMEM] + [VMEM] * 5 + [pl.BlockSpec(memory_space=HBM_SPACE)],
        "merge",
        scratch=[pltpu.VMEM(other.shape, BF16), pltpu.SemaphoreType.DMA((4,))],
        vmem=2 * VMEM_LIMIT,
    )(place, crossed, coeffs, other_coeffs, merge_mix, mine, other)

    got = [swap(pieces[i], "snap", 2 * i) for i in range(1, chips)]
    gram, low_rest, high_rest = call(
        rows_gram_kernel,
        (shape((5 * modes // 2, chips * modes), F32), rest, rest),
        [SMEM] + [VMEM] * (chips + 2),
        "rows_gram",
        scratch=[pltpu.VMEM((chips * modes, chunk), BF16)],
        aliases={chips + 1: 1, chips + 2: 2},
    )(place, pieces[0], *got, low_rest, high_rest)
    gram = odd_butterfly(butterfly(gram, "snap", (1,)), "snap", (2,))
    gram, far, low_rest, high_rest = lax.optimization_barrier((gram, pieces[0], low_rest, high_rest))
    far = swap(far, "snap", 4)
    low_rest = swap(low_rest, "snap", 2)
    high_rest = swap(high_rest, "snap", 6)
    gram = odd_butterfly(gram, "snap", (6,))
    gram = odd_butterfly(gram, "space", EARLY + LATE)

    whole = call(
        tree_kernel,
        shape((modes, chips * modes), F32),
        [SMEM] + [VMEM] * 3,
        "tree",
        21 * work // 10,
    )(place, gram, swap(gram, "snap", 1), merge_mix)
    half_out = shape((modes // snap_count, points // 2), F32)
    keep, give = call(
        finish_kernel,
        (half_out, half_out),
        [SMEM] + [VMEM] * (2 * chips + 3),
        "finish",
    )(place, whole, *pieces, *got, far, low_rest, high_rest)
    return call(
        assemble_kernel,
        shape((modes // snap_count, points), F32),
        [SMEM] + [VMEM] * 2,
        "assemble",
    )(place, keep, swap(give, "snap", 1))


def solution(mesh):
    in_specs = (P("snap", "space"), P(None, "snap"), P())
    out_specs = P("snap", "space")
    return jax.shard_map(shards, mesh=mesh, in_specs=in_specs, out_specs=out_specs, check_vma=False)
```

```python
import functools
import math

import jax
import jax.numpy as jnp
from jax import lax
from jax.experimental import pallas as pl
from jax.experimental.pallas import tpu as pltpu
from jax.sharding import PartitionSpec as P

ITERS = 4
PANEL = 8
F32 = jnp.float32
BF16 = jnp.bfloat16
VMEM_LIMIT = 24 * 1024 * 1024


def dot_nn(a, b):
    return jnp.dot(a, b, precision=lax.Precision.HIGHEST, preferred_element_type=F32)


def dot_nt(a, b):
    return lax.dot_general(
        a, b, (((1,), (1,)), ((), ())), precision=lax.Precision.HIGHEST, preferred_element_type=F32
    )


def dot_tn(a, b):
    return lax.dot_general(
        a, b, (((0,), (0,)), ((), ())), precision=lax.Precision.HIGHEST, preferred_element_type=F32
    )


def eliminate_panel(table, wide, first):
    group, inner = divmod(first, 8)
    shape = table[0].shape
    row_ids = lax.broadcasted_iota(jnp.int32, shape, 0)
    columns = [
        [jnp.broadcast_to(t[:, wide + first + k : wide + first + k + 1], shape) for t in table[group:]]
        for k in range(PANEL)
    ]
    rows = [jnp.broadcast_to(table[group][inner + k : inner + k + 1], shape) for k in range(PANEL)]
    corner = {
        (k, l): jnp.broadcast_to(columns[k][0][inner + l : inner + l + 1], shape)
        for k in range(PANEL)
        for l in range(k, PANEL)
    }
    for k in range(PANEL):
        inverse = 1.0 / corner[k, k]
        factors = [c * inverse for c in columns[k]]
        steps = {l: corner[k, l] * inverse for l in range(k + 1, PANEL)}
        for l in range(k + 1, PANEL):
            for m in range(l, PANEL):
                corner[l, m] = corner[l, m] - steps[l] * corner[k, m]
            columns[l] = [c - f * corner[k, l] for c, f in zip(columns[l], factors)]
            rows[l] = rows[l] - steps[l] * rows[k]
        factors[0] = jnp.where(row_ids > inner + k, factors[0], 0.0)
        for g, f in enumerate(factors):
            table[group + g] = table[group + g] - f * rows[k]


def cholesky_solves(pairs):
    modes = pairs[0][0].shape[0]
    wide = pairs[0][1].shape[1]
    tables = []
    for h, b in pairs:
        table = jnp.concatenate([b, h], axis=1)
        tables.append([table[r : r + 8] for r in range(0, modes, 8)])
    for first in range(0, modes, PANEL):
        for table in tables:
            eliminate_panel(table, wide, first)
    solved = []
    for table in tables:
        whole = jnp.concatenate(table, axis=0)
        below = whole[:, wide:]
        same = lax.broadcasted_iota(jnp.int32, below.shape, 0) == lax.broadcasted_iota(
            jnp.int32, below.shape, 1
        )
        diagonal = jnp.sum(jnp.where(same, below, 0.0), axis=1, keepdims=True)
        solved.append(whole[:, :wide] * lax.rsqrt(diagonal))
    return solved


def trace_scale(gram):
    same = lax.broadcasted_iota(jnp.int32, gram.shape, 0) == lax.broadcasted_iota(
        jnp.int32, gram.shape, 1
    )
    diagonal = jnp.where(same, gram, 0.0)
    return lax.rsqrt(jnp.sum(jnp.sum(diagonal, axis=1, keepdims=True), axis=0, keepdims=True))


def mixings(grams, mix):
    pairs = []
    for gram in grams:
        curved_t = dot_tn(mix, gram)
        pairs.append((dot_nn(curved_t, mix), curved_t))
    return [s * trace_scale(g) for s, g in zip(cholesky_solves(pairs), grams)]


def split_two(x):
    high = x.astype(BF16)
    return jnp.concatenate([high, (x - high.astype(F32)).astype(BF16)], axis=0)


def bf16_dot(a, b):
    return jnp.dot(a, b, preferred_element_type=F32)


def bf16_dot_nt(a, b):
    return lax.dot_general(a, b, (((1,), (1,)), ((), ())), preferred_element_type=F32)


def joined(both):
    modes = both.shape[0] // 2
    return both[:modes] + both[modes:]


def own_gram_kernel(place_ref, snaps_ref, gram_ref, mine_ref, away_ref, sems):
    core = place_ref[0]
    width, points = mine_ref.shape
    chips = sems.shape[0] // 2
    chunk = points // chips
    parts = []
    for packed_ref, parity in ((mine_ref, core), (away_ref, 1 - core)):
        copies = []
        for i in range(chips):
            there = pl.ds(pl.multiple_of((2 * i + parity) * chunk, chunk), chunk)
            here = pl.ds(i * chunk, chunk)
            sem = sems.at[len(parts) * chips + i]
            copies.append(pltpu.make_async_copy(snaps_ref.at[:, there], packed_ref.at[:, here], sem))
        parts.append((packed_ref, copies))
    for _, copies in parts:
        for copy in copies:
            copy.start()
    grams = []
    for packed_ref, copies in parts:
        for copy in copies:
            copy.wait()
        rows = packed_ref[...]
        grams.append(bf16_dot_nt(rows, rows))
    gram_ref[...] = jnp.zeros_like(gram_ref)
    gram_ref[:, :width] = grams[0] + grams[1]


def cross_gram_kernel(place_ref, mine_ref, other_ref, gram_ref):
    width = mine_ref.shape[0]
    gram_ref[...] = jnp.zeros_like(gram_ref)

    @pl.when(place_ref[0] == 0)
    def _():
        gram_ref[:, width:] = bf16_dot_nt(mine_ref[...], other_ref[...])

    @pl.when(place_ref[0] != 0)
    def _():
        gram_ref[:, width:] = bf16_dot_nt(other_ref[...], mine_ref[...])


def power_kernel(iters, last, gram_ref, coeffs_ref, out_ref):
    coeffs = coeffs_ref[...].astype(F32)
    width = coeffs.shape[1]
    modes = coeffs.shape[0]
    gram = gram_ref[:, :width]
    scale = 1.0 / math.sqrt(width)
    for _ in range(iters):
        weighted = dot_nn(coeffs, gram)
        solved = cholesky_solves([(dot_nt(weighted, coeffs), weighted)])[0]
        coeffs = solved.astype(BF16).astype(F32) * scale
    if last:
        out_ref[...] = jnp.zeros_like(out_ref)
        out_ref[:, :width] = coeffs
        out_ref[:, width : width + modes] = dot_nt(dot_nn(coeffs, gram), coeffs)
    else:
        out_ref[...] = coeffs


def stack_gram(low, cross, cross_t, high):
    return jnp.concatenate(
        [jnp.concatenate([low, cross], axis=1), jnp.concatenate([cross_t, high], axis=1)], axis=0
    )


def merge_kernel(place_ref, cross_ref, mine_co_ref, other_co_ref, mix_ref, mine_ref, other_hbm, *refs):
    out_refs, (other_ref, sem) = refs[:-2], refs[-2:]
    parts = sem.shape[0]
    part = other_ref.shape[0] // parts
    fetches = [
        pltpu.make_async_copy(other_hbm.at[pl.ds(i * part, part)], other_ref.at[pl.ds(i * part, part)], sem.at[i])
        for i in range(parts)
    ]
    for fetch in fetches:
        fetch.start()
    first = place_ref[0] == 0
    width = mine_ref.shape[0]
    modes = mine_co_ref.shape[0]
    mine_co, other_co = mine_co_ref[...], other_co_ref[...]
    low = jnp.where(first, mine_co, other_co)
    high = jnp.where(first, other_co, mine_co)
    low_co, high_co = low[:, :width], high[:, :width]
    cross = cross_ref[:, width:]
    gram = stack_gram(
        low[:, width : width + modes],
        dot_nt(dot_nn(low_co, cross), high_co),
        dot_nt(dot_nt(high_co, cross), low_co),
        high[:, width : width + modes],
    )
    mixing = mixings([gram], mix_ref[...])[0]
    low_mix = dot_nn(mixing[:, :modes], low_co)
    high_mix = dot_nn(mixing[:, modes:], high_co)
    mine_split = split_two(jnp.where(first, low_mix, high_mix))
    other_split = split_two(jnp.where(first, high_mix, low_mix))
    piece_refs, rest_refs = out_refs[:-2], out_refs[-2:]
    chunk = piece_refs[0].shape[1]
    split = jnp.concatenate([mine_split, other_split], axis=1)
    for fetch in fetches:
        fetch.wait()
    for i, piece_ref in enumerate(piece_refs):
        here = pl.ds(pl.multiple_of((place_ref[1] ^ i) * chunk, chunk), chunk)
        rows = jnp.concatenate([mine_ref[:, here], other_ref[:, here]], axis=0)
        piece = joined(bf16_dot(split, rows)).astype(BF16)
        piece_ref[...] = piece
        for rest_ref, slots in zip(rest_refs, REST_SLOTS):
            if i in slots:
                at = slots.index(i) * modes
                rest_ref[at : at + modes] = piece


NEIGHBOURS = (1, 3)
REST_SLOTS = ((0, 2, 3), (0, 1, 2))


def rows_gram_kernel(place_ref, *refs):
    piece_refs, (_, _, gram_ref, low_rest_ref, high_rest_ref, rows_ref) = refs[:-6], refs[-6:]
    modes = piece_refs[0].shape[0]
    low_rest_ref[3 * modes :] = piece_refs[3][...]
    high_rest_ref[3 * modes :] = piece_refs[1][...]
    for i, piece_ref in enumerate(piece_refs):
        start = pl.multiple_of((place_ref[1] ^ i) * modes, modes)
        rows_ref[pl.ds(start, modes), :] = piece_ref[...]
    rows = rows_ref[...]
    gram = bf16_dot_nt(rows, rows)
    m, h = modes, modes // 2
    gram_ref[:m] = gram[:m]
    gram_ref[m : 2 * m] = gram[m : 2 * m]
    gram_ref[m : 2 * m, :m] = gram[3 * m :, 3 * m :]
    gram_ref[2 * m :, : 2 * m] = gram[2 * m : 2 * m + h, 2 * m :]
    gram_ref[2 * m :, 2 * m :] = gram[2 * m + h : 3 * m, 2 * m :]


def tree_kernel(gram_ref, mix_ref, whole_ref):
    mix = mix_ref[...]
    m = mix.shape[1]
    h = m // 2
    top = gram_ref[:m]
    second = gram_ref[m : 2 * m]
    third = gram_ref[2 * m :]
    low = stack_gram(top[:, :m], top[:, m : 2 * m], top[:, m : 2 * m].T, second[:, m : 2 * m])
    third = jnp.concatenate([third[:, : 2 * m], third[:, 2 * m :]], axis=0)
    high = stack_gram(third[:, :m], third[:, m:], third[:, m:].T, second[:, :m])
    cross = jnp.concatenate([top[:, 2 * m :], second[:, 2 * m :]], axis=0)
    low_mix, high_mix = mixings([low, high], mix)
    gram = stack_gram(
        dot_nt(dot_nn(low_mix, low), low_mix),
        dot_nt(dot_nn(low_mix, cross), high_mix),
        dot_nt(dot_nt(high_mix, cross), low_mix),
        dot_nt(dot_nn(high_mix, high), high_mix),
    )
    last = mixings([gram], mix)[0]
    whole_ref[...] = jnp.concatenate(
        [dot_nn(last[:, :m], low_mix), dot_nn(last[:, m:], high_mix)], axis=1
    )


def finish_kernel(place_ref, whole_ref, *refs):
    own_refs, got_refs = refs[:4], refs[4:7]
    far_ref, low_rest_ref, high_rest_ref, keep_ref, give_ref = refs[7:]
    chips = len(own_refs)
    core, chip = place_ref[0], place_ref[1]
    modes, chunk = own_refs[0].shape
    own = 2 * keep_ref.shape[0]
    mixing = whole_ref[pl.ds(pl.multiple_of(chip * own, own), own), :]
    mixing = jnp.where(chip & 2 != 0, pltpu.roll(mixing, 2 * modes, 1), mixing)
    lanes = lax.broadcasted_iota(jnp.int32, mixing.shape, 1)
    turned = jnp.where(
        (lanes // modes) % 2 == 0,
        pltpu.roll(mixing, (chips - 1) * modes, 1),
        pltpu.roll(mixing, modes, 1),
    )
    split = split_two(jnp.where(chip & 1 != 0, turned, mixing))
    for r in range(chips):
        blocks = [own_refs[r][...]]
        if r == 0:
            blocks += [got_ref[...] for got_ref in got_refs]
        else:
            near = [
                rest_ref[slots.index(apart ^ r) * modes : (slots.index(apart ^ r) + 1) * modes]
                for rest_ref, slots, apart in zip((low_rest_ref, high_rest_ref), REST_SLOTS, NEIGHBOURS)
            ]
            far = {1: low_rest_ref[3 * modes :], 2: far_ref[...], 3: high_rest_ref[3 * modes :]}[r]
            blocks += [near[0], far, near[1]]
        part = joined(bf16_dot(split, jnp.concatenate(blocks, axis=0)))
        low, high = part[: own // 2], part[own // 2 :]
        there = pl.ds(pl.multiple_of((chip ^ r) * chunk, chunk), chunk)
        keep_ref[:, there] = jnp.where(core == 0, low, high)
        give_ref[:, there] = jnp.where(core == 0, high, low)


def assemble_kernel(place_ref, keep_ref, got_ref, out_ref):
    core = place_ref[0]
    chips = out_ref.shape[1] // keep_ref.shape[1] * 2
    chunk = keep_ref.shape[1] // chips
    for i in range(chips):
        here = pl.ds(i * chunk, chunk)
        out_ref[:, pl.ds(pl.multiple_of((2 * i + core) * chunk, chunk), chunk)] = keep_ref[:, here]
        out_ref[:, pl.ds(pl.multiple_of((2 * i + 1 - core) * chunk, chunk), chunk)] = got_ref[:, here]


VMEM = pl.BlockSpec(memory_space=pltpu.VMEM)
SMEM = pl.BlockSpec(memory_space=pltpu.SMEM)
HBM_SPACE = pltpu.HBM


def call(kernel, out_shape, in_specs, name, flops=0, scratch=(), vmem=VMEM_LIMIT, aliases=()):
    return pl.pallas_call(
        kernel,
        out_shape=out_shape,
        in_specs=in_specs,
        out_specs=jax.tree.map(lambda _: VMEM, out_shape),
        scratch_shapes=scratch,
        input_output_aliases=dict(aliases),
        compiler_params=pltpu.CompilerParams(vmem_limit_bytes=vmem),
        cost_estimate=pl.CostEstimate(flops=flops, bytes_accessed=0, transcendentals=0),
        name=name,
    )


def swap(block, axis, mask):
    count = lax.axis_size(axis)
    return lax.ppermute(block, axis, [(i, i ^ mask) for i in range(count)])


def butterfly(block, axis, masks):
    for mask in masks:
        block = block + swap(block, axis, mask)
    return block


EARLY = (1, 4)
LATE = (3, 8, 24)


def shards(snaps, sketch, merge_mix):
    width, points = snaps.shape
    modes = sketch.shape[0]
    snap_count = lax.axis_size("snap")
    chunk = points // snap_count
    chips = snap_count // 2
    position = lax.axis_index("snap")
    place = jnp.stack([position % 2, position // 2]).astype(jnp.int32)
    shape = jax.ShapeDtypeStruct

    own_gram, mine, away = call(
        own_gram_kernel,
        (shape((width, 2 * width), F32),) + (shape((width, chips * chunk), snaps.dtype),) * 2,
        [SMEM, pl.BlockSpec(memory_space=HBM_SPACE)],
        "own_gram",
        scratch=[pltpu.SemaphoreType.DMA((2 * chips,))],
        vmem=2 * VMEM_LIMIT,
    )(place, snaps)
    other = swap(away, "snap", 1)
    own_gram = butterfly(own_gram, "space", EARLY)

    cross = call(
        cross_gram_kernel,
        shape((width, 2 * width), F32),
        [SMEM] + [VMEM] * 2,
        "cross_gram",
    )(place, mine, other)
    cross = butterfly(cross, "snap", (1,))
    grams = butterfly(own_gram + cross, "space", LATE)
    crossed = butterfly(grams, "space", EARLY)

    work = 4 * 10**9
    half = call(
        functools.partial(power_kernel, ITERS // 2, False),
        shape((modes, width), F32),
        [VMEM] * 2,
        "power_first",
        work,
    )(grams, sketch)
    coeffs = call(
        functools.partial(power_kernel, ITERS - ITERS // 2, True),
        shape((modes, 2 * width), F32),
        [VMEM] * 2,
        "power_last",
        work,
    )(grams, half)
    other_coeffs = swap(coeffs, "snap", 1)

    piece = shape((modes, chunk), BF16)
    rest = shape((4 * modes, chunk), BF16)
    *pieces, low_rest, high_rest = call(
        merge_kernel,
        (piece,) * chips + (rest,) * 2,
        [SMEM] + [VMEM] * 5 + [pl.BlockSpec(memory_space=HBM_SPACE)],
        "merge",
        scratch=[pltpu.VMEM(other.shape, BF16), pltpu.SemaphoreType.DMA((4,))],
        vmem=2 * VMEM_LIMIT,
    )(place, crossed, coeffs, other_coeffs, merge_mix, mine, other)

    got = [swap(pieces[i], "snap", 2 * i) for i in range(1, chips)]
    far, got[0] = lax.optimization_barrier((pieces[0], got[0]))
    far = swap(far, "snap", 4)
    gram, low_rest, high_rest = call(
        rows_gram_kernel,
        (shape((5 * modes // 2, chips * modes), F32), rest, rest),
        [SMEM] + [VMEM] * (chips + 2),
        "rows_gram",
        scratch=[pltpu.VMEM((chips * modes, chunk), BF16)],
        aliases={chips + 1: 1, chips + 2: 2},
    )(place, pieces[0], *got, low_rest, high_rest)
    gram = butterfly(gram, "snap", (1, 2))
    gram, far, low_rest, high_rest = lax.optimization_barrier((gram, far, low_rest, high_rest))
    low_rest = swap(low_rest, "snap", 2)
    high_rest = swap(high_rest, "snap", 6)
    gram = butterfly(gram, "snap", (6,))
    gram = butterfly(gram, "space", EARLY + LATE)

    whole = call(
        tree_kernel, shape((modes, chips * modes), F32), [VMEM] * 2, "tree", 22 * work // 10
    )(gram, merge_mix)
    half_out = shape((modes // snap_count, points // 2), F32)
    keep, give = call(
        finish_kernel,
        (half_out, half_out),
        [SMEM] + [VMEM] * (2 * chips + 3),
        "finish",
    )(place, whole, *pieces, *got, far, low_rest, high_rest)
    return call(
        assemble_kernel,
        shape((modes // snap_count, points), F32),
        [SMEM] + [VMEM] * 2,
        "assemble",
    )(place, keep, swap(give, "snap", 1))


def solution(mesh):
    in_specs = (P("snap", "space"), P(None, "snap"), P())
    out_specs = P("snap", "space")
    return jax.shard_map(shards, mesh=mesh, in_specs=in_specs, out_specs=out_specs, check_vma=False)
```

```python
import functools
import math

import jax
import jax.numpy as jnp
from jax import lax
from jax.experimental import pallas as pl
from jax.experimental.pallas import tpu as pltpu
from jax.sharding import PartitionSpec as P

ITERS = 4
PANEL = 8
F32 = jnp.float32
BF16 = jnp.bfloat16
VMEM_LIMIT = 24 * 1024 * 1024


def dot_nn(a, b):
    return jnp.dot(a, b, precision=lax.Precision.HIGHEST, preferred_element_type=F32)


def dot_nt(a, b):
    return lax.dot_general(
        a, b, (((1,), (1,)), ((), ())), precision=lax.Precision.HIGHEST, preferred_element_type=F32
    )


def dot_tn(a, b):
    return lax.dot_general(
        a, b, (((0,), (0,)), ((), ())), precision=lax.Precision.HIGHEST, preferred_element_type=F32
    )


def eliminate_panel(table, wide, first):
    group, inner = divmod(first, 8)
    shape = table[0].shape
    row_ids = lax.broadcasted_iota(jnp.int32, shape, 0)
    columns = [
        [jnp.broadcast_to(t[:, wide + first + k : wide + first + k + 1], shape) for t in table[group:]]
        for k in range(PANEL)
    ]
    rows = [jnp.broadcast_to(table[group][inner + k : inner + k + 1], shape) for k in range(PANEL)]
    corner = {
        (k, l): jnp.broadcast_to(columns[k][0][inner + l : inner + l + 1], shape)
        for k in range(PANEL)
        for l in range(k, PANEL)
    }
    for k in range(PANEL):
        inverse = 1.0 / corner[k, k]
        factors = [c * inverse for c in columns[k]]
        steps = {l: corner[k, l] * inverse for l in range(k + 1, PANEL)}
        for l in range(k + 1, PANEL):
            for m in range(l, PANEL):
                corner[l, m] = corner[l, m] - steps[l] * corner[k, m]
            columns[l] = [c - f * corner[k, l] for c, f in zip(columns[l], factors)]
            rows[l] = rows[l] - steps[l] * rows[k]
        factors[0] = jnp.where(row_ids > inner + k, factors[0], 0.0)
        for g, f in enumerate(factors):
            table[group + g] = table[group + g] - f * rows[k]


def cholesky_solves(pairs):
    modes = pairs[0][0].shape[0]
    wide = pairs[0][1].shape[1]
    tables = []
    for h, b in pairs:
        table = jnp.concatenate([b, h], axis=1)
        tables.append([table[r : r + 8] for r in range(0, modes, 8)])
    for first in range(0, modes, PANEL):
        for table in tables:
            eliminate_panel(table, wide, first)
    solved = []
    for table in tables:
        whole = jnp.concatenate(table, axis=0)
        below = whole[:, wide:]
        same = lax.broadcasted_iota(jnp.int32, below.shape, 0) == lax.broadcasted_iota(
            jnp.int32, below.shape, 1
        )
        diagonal = jnp.sum(jnp.where(same, below, 0.0), axis=1, keepdims=True)
        solved.append(whole[:, :wide] * lax.rsqrt(diagonal))
    return solved


def trace_scale(gram):
    same = lax.broadcasted_iota(jnp.int32, gram.shape, 0) == lax.broadcasted_iota(
        jnp.int32, gram.shape, 1
    )
    diagonal = jnp.where(same, gram, 0.0)
    return lax.rsqrt(jnp.sum(jnp.sum(diagonal, axis=1, keepdims=True), axis=0, keepdims=True))


def mixings(grams, mix):
    pairs = []
    for gram in grams:
        curved_t = dot_tn(mix, gram)
        pairs.append((dot_nn(curved_t, mix), curved_t))
    return [s * trace_scale(g) for s, g in zip(cholesky_solves(pairs), grams)]


def split_two(x):
    high = x.astype(BF16)
    return jnp.concatenate([high, (x - high.astype(F32)).astype(BF16)], axis=0)


def bf16_dot(a, b):
    return jnp.dot(a, b, preferred_element_type=F32)


def bf16_dot_nt(a, b):
    return lax.dot_general(a, b, (((1,), (1,)), ((), ())), preferred_element_type=F32)


def joined(both):
    modes = both.shape[0] // 2
    return both[:modes] + both[modes:]


def own_gram_kernel(place_ref, snaps_ref, gram_ref, mine_ref, away_ref, sems):
    core = place_ref[0]
    width, points = mine_ref.shape
    chips = sems.shape[0] // 2
    chunk = points // chips
    parts = []
    for packed_ref, parity in ((mine_ref, core), (away_ref, 1 - core)):
        copies = []
        for i in range(chips):
            there = pl.ds(pl.multiple_of((2 * i + parity) * chunk, chunk), chunk)
            here = pl.ds(i * chunk, chunk)
            sem = sems.at[len(parts) * chips + i]
            copies.append(pltpu.make_async_copy(snaps_ref.at[:, there], packed_ref.at[:, here], sem))
        parts.append((packed_ref, copies))
    for _, copies in parts:
        for copy in copies:
            copy.start()
    grams = []
    for packed_ref, copies in parts:
        for copy in copies:
            copy.wait()
        rows = packed_ref[...]
        grams.append(bf16_dot_nt(rows, rows))
    gram_ref[...] = jnp.zeros_like(gram_ref)
    gram_ref[:, :width] = grams[0] + grams[1]


def cross_gram_kernel(place_ref, mine_ref, other_ref, gram_ref):
    width = mine_ref.shape[0]
    gram_ref[...] = jnp.zeros_like(gram_ref)

    @pl.when(place_ref[0] == 0)
    def _():
        gram_ref[:, width:] = bf16_dot_nt(mine_ref[...], other_ref[...])

    @pl.when(place_ref[0] != 0)
    def _():
        gram_ref[:, width:] = bf16_dot_nt(other_ref[...], mine_ref[...])


def power_kernel(iters, last, gram_ref, coeffs_ref, out_ref):
    coeffs = coeffs_ref[...].astype(F32)
    width = coeffs.shape[1]
    modes = coeffs.shape[0]
    gram = gram_ref[:, :width]
    scale = 1.0 / math.sqrt(width)
    for _ in range(iters):
        weighted = dot_nn(coeffs, gram)
        solved = cholesky_solves([(dot_nt(weighted, coeffs), weighted)])[0]
        coeffs = solved.astype(BF16).astype(F32) * scale
    if last:
        out_ref[...] = jnp.zeros_like(out_ref)
        out_ref[:, :width] = coeffs
        out_ref[:, width : width + modes] = dot_nt(dot_nn(coeffs, gram), coeffs)
    else:
        out_ref[...] = coeffs


def stack_gram(low, cross, cross_t, high):
    return jnp.concatenate(
        [jnp.concatenate([low, cross], axis=1), jnp.concatenate([cross_t, high], axis=1)], axis=0
    )


def merge_kernel(place_ref, cross_ref, mine_co_ref, other_co_ref, mix_ref, mine_ref, other_hbm, *refs):
    out_refs, (other_ref, sem) = refs[:-2], refs[-2:]
    chunk = out_refs[0].shape[1]
    fetches = []
    for i in range(sem.shape[0]):
        there = pl.ds(pl.multiple_of((place_ref[1] ^ i) * chunk, chunk), chunk)
        slot = other_ref.at[:, pl.ds(i * chunk, chunk)]
        fetches.append(pltpu.make_async_copy(other_hbm.at[:, there], slot, sem.at[i]))
    for fetch in fetches:
        fetch.start()
    first = place_ref[0] == 0
    width = mine_ref.shape[0]
    modes = mine_co_ref.shape[0]
    mine_co, other_co = mine_co_ref[...], other_co_ref[...]
    low = jnp.where(first, mine_co, other_co)
    high = jnp.where(first, other_co, mine_co)
    low_co, high_co = low[:, :width], high[:, :width]
    cross = cross_ref[:, width:]
    gram = stack_gram(
        low[:, width : width + modes],
        dot_nt(dot_nn(low_co, cross), high_co),
        dot_nt(dot_nt(high_co, cross), low_co),
        high[:, width : width + modes],
    )
    mixing = mixings([gram], mix_ref[...])[0]
    low_mix = dot_nn(mixing[:, :modes], low_co)
    high_mix = dot_nn(mixing[:, modes:], high_co)
    mine_split = split_two(jnp.where(first, low_mix, high_mix))
    other_split = split_two(jnp.where(first, high_mix, low_mix))
    piece_refs, rest_refs = out_refs[:-2], out_refs[-2:]
    split = jnp.concatenate([mine_split, other_split], axis=1)
    for i, piece_ref in enumerate(piece_refs):
        if i % 2 == 0:
            fetches[i].wait()
            fetches[i + 1].wait()
        here = pl.ds(pl.multiple_of((place_ref[1] ^ i) * chunk, chunk), chunk)
        rows = jnp.concatenate([mine_ref[:, here], other_ref[:, i * chunk : (i + 1) * chunk]], axis=0)
        piece = joined(bf16_dot(split, rows)).astype(BF16)
        piece_ref[...] = piece
        for rest_ref, slots in zip(rest_refs, REST_SLOTS):
            if i in slots:
                at = slots.index(i) * modes
                rest_ref[at : at + modes] = piece


NEIGHBOURS = (1, 3)
REST_SLOTS = ((0, 2, 3), (0, 1, 2))


def rows_gram_kernel(place_ref, *refs):
    piece_refs, (_, _, gram_ref, low_rest_ref, high_rest_ref, rows_ref) = refs[:-6], refs[-6:]
    modes = piece_refs[0].shape[0]
    low_rest_ref[3 * modes :] = piece_refs[3][...]
    high_rest_ref[3 * modes :] = piece_refs[1][...]
    for i, piece_ref in enumerate(piece_refs):
        start = pl.multiple_of((place_ref[1] ^ i) * modes, modes)
        rows_ref[pl.ds(start, modes), :] = piece_ref[...]
    rows = rows_ref[...]
    gram = bf16_dot_nt(rows, rows)
    m, h = modes, modes // 2
    gram_ref[:m] = gram[:m]
    gram_ref[m : 2 * m] = gram[m : 2 * m]
    gram_ref[m : 2 * m, :m] = gram[3 * m :, 3 * m :]
    gram_ref[2 * m :, : 2 * m] = gram[2 * m : 2 * m + h, 2 * m :]
    gram_ref[2 * m :, 2 * m :] = gram[2 * m + h : 3 * m, 2 * m :]


def tree_kernel(gram_ref, mix_ref, whole_ref):
    mix = mix_ref[...]
    m = mix.shape[1]
    h = m // 2
    top = gram_ref[:m]
    second = gram_ref[m : 2 * m]
    third = gram_ref[2 * m :]
    low = stack_gram(top[:, :m], top[:, m : 2 * m], top[:, m : 2 * m].T, second[:, m : 2 * m])
    third = jnp.concatenate([third[:, : 2 * m], third[:, 2 * m :]], axis=0)
    high = stack_gram(third[:, :m], third[:, m:], third[:, m:].T, second[:, :m])
    cross = jnp.concatenate([top[:, 2 * m :], second[:, 2 * m :]], axis=0)
    low_mix, high_mix = mixings([low, high], mix)
    gram = stack_gram(
        dot_nt(dot_nn(low_mix, low), low_mix),
        dot_nt(dot_nn(low_mix, cross), high_mix),
        dot_nt(dot_nt(high_mix, cross), low_mix),
        dot_nt(dot_nn(high_mix, high), high_mix),
    )
    last = mixings([gram], mix)[0]
    whole_ref[...] = jnp.concatenate(
        [dot_nn(last[:, :m], low_mix), dot_nn(last[:, m:], high_mix)], axis=1
    )


def finish_kernel(place_ref, whole_ref, *refs):
    own_refs, got_refs = refs[:4], refs[4:7]
    far_ref, low_rest_ref, high_rest_ref, keep_ref, give_ref = refs[7:]
    chips = len(own_refs)
    core, chip = place_ref[0], place_ref[1]
    modes, chunk = own_refs[0].shape
    own = 2 * keep_ref.shape[0]
    mixing = whole_ref[pl.ds(pl.multiple_of(chip * own, own), own), :]
    mixing = jnp.where(chip & 2 != 0, pltpu.roll(mixing, 2 * modes, 1), mixing)
    lanes = lax.broadcasted_iota(jnp.int32, mixing.shape, 1)
    turned = jnp.where(
        (lanes // modes) % 2 == 0,
        pltpu.roll(mixing, (chips - 1) * modes, 1),
        pltpu.roll(mixing, modes, 1),
    )
    split = split_two(jnp.where(chip & 1 != 0, turned, mixing))
    for r in range(chips):
        blocks = [own_refs[r][...]]
        if r == 0:
            blocks += [got_ref[...] for got_ref in got_refs]
        else:
            near = [
                rest_ref[slots.index(apart ^ r) * modes : (slots.index(apart ^ r) + 1) * modes]
                for rest_ref, slots, apart in zip((low_rest_ref, high_rest_ref), REST_SLOTS, NEIGHBOURS)
            ]
            far = {1: low_rest_ref[3 * modes :], 2: far_ref[...], 3: high_rest_ref[3 * modes :]}[r]
            blocks += [near[0], far, near[1]]
        part = joined(bf16_dot(split, jnp.concatenate(blocks, axis=0)))
        low, high = part[: own // 2], part[own // 2 :]
        there = pl.ds(pl.multiple_of((chip ^ r) * chunk, chunk), chunk)
        keep_ref[:, there] = jnp.where(core == 0, low, high)
        give_ref[:, there] = jnp.where(core == 0, high, low)


def assemble_kernel(place_ref, keep_ref, got_ref, out_ref):
    core = place_ref[0]
    chips = out_ref.shape[1] // keep_ref.shape[1] * 2
    chunk = keep_ref.shape[1] // chips
    for i in range(chips):
        here = pl.ds(i * chunk, chunk)
        out_ref[:, pl.ds(pl.multiple_of((2 * i + core) * chunk, chunk), chunk)] = keep_ref[:, here]
        out_ref[:, pl.ds(pl.multiple_of((2 * i + 1 - core) * chunk, chunk), chunk)] = got_ref[:, here]


VMEM = pl.BlockSpec(memory_space=pltpu.VMEM)
SMEM = pl.BlockSpec(memory_space=pltpu.SMEM)
HBM_SPACE = pltpu.HBM


def call(kernel, out_shape, in_specs, name, flops=0, scratch=(), vmem=VMEM_LIMIT, aliases=()):
    return pl.pallas_call(
        kernel,
        out_shape=out_shape,
        in_specs=in_specs,
        out_specs=jax.tree.map(lambda _: VMEM, out_shape),
        scratch_shapes=scratch,
        input_output_aliases=dict(aliases),
        compiler_params=pltpu.CompilerParams(vmem_limit_bytes=vmem),
        cost_estimate=pl.CostEstimate(flops=flops, bytes_accessed=0, transcendentals=0),
        name=name,
    )


def swap(block, axis, mask):
    count = lax.axis_size(axis)
    return lax.ppermute(block, axis, [(i, i ^ mask) for i in range(count)])


def butterfly(block, axis, masks):
    for mask in masks:
        block = block + swap(block, axis, mask)
    return block


EARLY = (1, 4)
LATE = (3, 8, 24)


def shards(snaps, sketch, merge_mix):
    width, points = snaps.shape
    modes = sketch.shape[0]
    snap_count = lax.axis_size("snap")
    chunk = points // snap_count
    chips = snap_count // 2
    position = lax.axis_index("snap")
    place = jnp.stack([position % 2, position // 2]).astype(jnp.int32)
    shape = jax.ShapeDtypeStruct

    own_gram, mine, away = call(
        own_gram_kernel,
        (shape((width, 2 * width), F32),) + (shape((width, chips * chunk), snaps.dtype),) * 2,
        [SMEM, pl.BlockSpec(memory_space=HBM_SPACE)],
        "own_gram",
        scratch=[pltpu.SemaphoreType.DMA((2 * chips,))],
        vmem=2 * VMEM_LIMIT,
    )(place, snaps)
    other = swap(away, "snap", 1)
    own_gram = butterfly(own_gram, "space", EARLY)

    cross = call(
        cross_gram_kernel,
        shape((width, 2 * width), F32),
        [SMEM] + [VMEM] * 2,
        "cross_gram",
    )(place, mine, other)
    cross = butterfly(cross, "snap", (1,))
    grams = butterfly(own_gram + cross, "space", LATE)
    crossed = butterfly(grams, "space", EARLY)

    work = 4 * 10**9
    half = call(
        functools.partial(power_kernel, ITERS // 2, False),
        shape((modes, width), F32),
        [VMEM] * 2,
        "power_first",
        work,
    )(grams, sketch)
    coeffs = call(
        functools.partial(power_kernel, ITERS - ITERS // 2, True),
        shape((modes, 2 * width), F32),
        [VMEM] * 2,
        "power_last",
        work,
    )(grams, half)
    other_coeffs = swap(coeffs, "snap", 1)

    piece = shape((modes, chunk), BF16)
    rest = shape((4 * modes, chunk), BF16)
    *pieces, low_rest, high_rest = call(
        merge_kernel,
        (piece,) * chips + (rest,) * 2,
        [SMEM] + [VMEM] * 5 + [pl.BlockSpec(memory_space=HBM_SPACE)],
        "merge",
        scratch=[pltpu.VMEM(other.shape, BF16), pltpu.SemaphoreType.DMA((4,))],
        vmem=2 * VMEM_LIMIT,
    )(place, crossed, coeffs, other_coeffs, merge_mix, mine, other)

    got = [swap(pieces[i], "snap", 2 * i) for i in range(1, chips)]
    gram, low_rest, high_rest = call(
        rows_gram_kernel,
        (shape((5 * modes // 2, chips * modes), F32), rest, rest),
        [SMEM] + [VMEM] * (chips + 2),
        "rows_gram",
        scratch=[pltpu.VMEM((chips * modes, chunk), BF16)],
        aliases={chips + 1: 1, chips + 2: 2},
    )(place, pieces[0], *got, low_rest, high_rest)
    gram = butterfly(gram, "snap", (1, 2))
    gram, far, low_rest, high_rest = lax.optimization_barrier((gram, pieces[0], low_rest, high_rest))
    far = swap(far, "snap", 4)
    low_rest = swap(low_rest, "snap", 2)
    high_rest = swap(high_rest, "snap", 6)
    gram = butterfly(gram, "snap", (6,))
    gram = butterfly(gram, "space", EARLY + LATE)

    whole = call(
        tree_kernel, shape((modes, chips * modes), F32), [VMEM] * 2, "tree", 22 * work // 10
    )(gram, merge_mix)
    half_out = shape((modes // snap_count, points // 2), F32)
    keep, give = call(
        finish_kernel,
        (half_out, half_out),
        [SMEM] + [VMEM] * (2 * chips + 3),
        "finish",
    )(place, whole, *pieces, *got, far, low_rest, high_rest)
    return call(
        assemble_kernel,
        shape((modes // snap_count, points), F32),
        [SMEM] + [VMEM] * 2,
        "assemble",
    )(place, keep, swap(give, "snap", 1))


def solution(mesh):
    in_specs = (P("snap", "space"), P(None, "snap"), P())
    out_specs = P("snap", "space")
    return jax.shard_map(shards, mesh=mesh, in_specs=in_specs, out_specs=out_specs, check_vma=False)
```
